512 devices in a mesh: enc: 64 (over x, z), dec: 8 (over y, core).
Axes of the slice: x: 4, y: 4, z: 16, core: 2. Of those that a mesh axis runs over, the one named last changes fastest.
Arguments:
- pixels: bfloat16 [8, 576, 3072], P('dec', 'enc'), may hold values from -6 to 6
- tile_counts: int32 [8, 64], P('dec', 'enc'), may hold values from 1 to 9, as said below
- text_gaps: int32 [8, 64], P('dec', 'enc'), may hold values from 0 to 64
- stem_weight: bfloat16 [48, 384], replicated, may hold values from -0.875 to 0.875
- depth_weight: bfloat16 [49, 384], replicated, may hold values from -0.875 to 0.875
- norm_gain: float32 [384], replicated, may hold values from 0.5 to 2
- up_weight: bfloat16 [384, 768], replicated, may hold values from -0.3125 to 0.3125
- down_weight: bfloat16 [768, 384], replicated, may hold values from -0.21875 to 0.21875
- layer_scale: float32 [384], replicated, may hold values from 0.25 to 1
- embed_grad: bfloat16 [64, 1664, 384], P('enc', 'dec'), may hold values from -6 to 6
Outputs:
- image_embeds: bfloat16 [64, 1664, 384], P('enc', 'dec')
- stem_grad: float32 [48, 384], replicated
- depth_grad: float32 [49, 384], replicated
- gain_grad: float32 [384], replicated
- up_grad: float32 [384, 768], replicated
- down_grad: float32 [768, 384], replicated
- scale_grad: float32 [384], replicated
The draws below stay inside these ranges and needn't reach their ends.
Inputs may be any that keep to these rules, and one draw needn't show every extreme that they name: `tile_counts`: for each index of dec, the counts of each aligned group of four consecutive indices of enc sum to exactly 12.
All inputs are finite; a program needn't handle non-finite values.
Results may differ from the reference program's by a relative error of at most 0.013.
Values may be sent and summed in bfloat16 or wider, within the bound.
No kernel may reach another device: no remote copies, remote signals or barrier semaphores. Data moves between devices by JAX's collectives and lax.ppermute only.
A program may use at most 64 MiB of HBM per device.

```python
import math
import jax
import jax.numpy as jnp
from jax import lax

WIDTH = 384
INNER = 768
KERNEL = 7
PATCH_CH = 48
TILE = 8
GAP = 64
MEAN_TILES = 3
SLOTS = 9
PIX = 3072
FEAT_TILE = 16
ENC_TILES = 576
SEQ = 1664
N_ENC = 64
N_DEC = 8


def draw_tile_counts(key, part):
    key = jax.random.fold_in(key, 7)
    keys = jax.random.split(key, 5)
    group_total = N_ENC // 4
    forced = jax.random.randint(keys[0], (N_DEC, 1), 0, group_total)
    is_forced = jnp.arange(group_total)[None, :] == forced
    largest = jax.random.randint(keys[1], (N_DEC, group_total), MEAN_TILES, 3 * MEAN_TILES + 1)
    largest = jnp.where(is_forced, 3 * MEAN_TILES, largest)
    remainder = 4 * MEAN_TILES - largest
    first_part = jax.random.randint(keys[2], (N_DEC, group_total), 1, remainder - 1)
    first_part = jnp.where(is_forced, 1, first_part)
    second_part = jax.random.randint(keys[3], (N_DEC, group_total), 1, remainder - first_part)
    third_part = remainder - first_part - second_part
    grouped = jnp.stack([largest, first_part, second_part, third_part], axis=2)
    order_keys = jax.random.split(keys[4], N_DEC * group_total)
    orders = jax.vmap(lambda one_key: jax.random.permutation(one_key, 4))(order_keys).reshape(N_DEC, group_total, 4)
    mixed = jnp.take_along_axis(grouped, orders, axis=2)
    return mixed.reshape(N_DEC, N_ENC).astype(jnp.int32)


def set_ends(result, stream_key, low, high):
    longest = result.shape.index(max(result.shape))
    spots = []
    for shift in (0, 1):
        where = [jax.random.randint(jax.random.fold_in(stream_key, axis), (), 0, length) for axis, length in enumerate(result.shape)]
        where[longest] = (where[longest] + shift) % result.shape[longest]
        spots.append(tuple(where))
    return result.at[spots[0]].set(low).at[spots[1]].set(high)


def shard_levels(own_key, shape, pieces, least, high):
    loudness, own = 1.0, jax.random.fold_in(own_key, 6)
    for dim, blocks in pieces:
        draws = jnp.exp(jax.random.uniform(jax.random.fold_in(own, dim), (blocks,), jnp.float32, least / len(pieces), high / len(pieces)))
        loudness = loudness * jnp.repeat(draws, shape[dim] // blocks).reshape([-1 if axis == dim else 1 for axis in range(len(shape))])
    return loudness


def noise(stream_key, shape, width, limit, cuts=(), kind=jnp.bfloat16):
    gain = shard_levels(stream_key, shape, cuts, -0.22, 0.18) if cuts else 1.0
    drawn = jax.random.normal(stream_key, shape, jnp.float32) * width * gain
    return jnp.minimum(jnp.maximum(drawn, -limit), limit).astype(kind)


def setup_inputs(seed: int = 0) -> dict:
    streams_of = jax.random.split(jax.random.key(seed), 11)
    pixels = noise(streams_of[0], (N_DEC, ENC_TILES, PIX), 1.0, 6.0, ((0, 8), (1, 64)))
    tile_counts = draw_tile_counts(jax.random.fold_in(streams_of[10], 71), 0)
    text_gaps = set_ends(jax.random.randint(streams_of[2], (N_DEC, N_ENC), 0, GAP + 1), jax.random.fold_in(streams_of[2], 1), 0, GAP).astype(jnp.int32)
    stem_weight = noise(streams_of[3], (PATCH_CH, WIDTH), PATCH_CH ** -0.5, 0.875)
    depth_weight = noise(streams_of[4], (KERNEL * KERNEL, WIDTH), (KERNEL * KERNEL) ** -0.5, 0.875)
    norm_gain = jnp.clip(jnp.exp(jax.random.uniform(streams_of[5], (WIDTH,), jnp.float32, math.log(0.5), math.log(2.0))), 0.5, 2.0)
    up_weight = noise(streams_of[6], (WIDTH, INNER), WIDTH ** -0.5, 0.3125)
    down_weight = noise(streams_of[7], (INNER, WIDTH), INNER ** -0.5, 0.21875)
    layer_scale = jnp.clip(jnp.exp(jax.random.uniform(streams_of[8], (WIDTH,), jnp.float32, math.log(0.25), math.log(1.0))), 0.25, 1.0)
    embed_grad = noise(streams_of[9], (N_ENC, SEQ, WIDTH), 1.0, 6.0, ((0, 64), (1, 8)))
    return dict(pixels=pixels, tile_counts=tile_counts, text_gaps=text_gaps, stem_weight=stem_weight, depth_weight=depth_weight, norm_gain=norm_gain, up_weight=up_weight, down_weight=down_weight, layer_scale=layer_scale, embed_grad=embed_grad)


epsilon = 1e-06

def encode(tile_block, stem_weight, depth_weight, norm_gain, up_weight, down_weight, layer_scale):
    tile_total = tile_block.shape[0]
    reach = KERNEL // 2
    half_tile = TILE // 2
    patches = tile_block.reshape(tile_total * TILE * TILE, PATCH_CH)
    stem_out = jnp.dot(patches, stem_weight, preferred_element_type=jnp.float32).astype(jnp.bfloat16)
    stem_grid = stem_out.reshape(tile_total, TILE, TILE, WIDTH).astype(jnp.float32)
    padded = jnp.pad(stem_grid, ((0, 0), (reach, reach), (reach, reach), (0, 0)))
    kernel = depth_weight.astype(jnp.float32)
    mixed_field = jnp.zeros_like(stem_grid)
    for row_tap in range(KERNEL):
        for col_tap in range(KERNEL):
            mixed_field = mixed_field + padded[:, row_tap:row_tap + TILE, col_tap:col_tap + TILE, :] * kernel[row_tap * KERNEL + col_tap]
    flat_rows = mixed_field.reshape(-1, WIDTH)
    channel_mean = lax.optimization_barrier(jnp.mean(flat_rows, axis=1, keepdims=True))
    deviation = flat_rows - channel_mean
    variance = lax.optimization_barrier(jnp.mean(deviation * deviation, axis=1, keepdims=True))
    inv_std = lax.rsqrt(variance + epsilon)
    centred = deviation * inv_std
    normed = (centred * norm_gain).astype(jnp.bfloat16)
    hidden = jnp.dot(normed, up_weight, preferred_element_type=jnp.float32)
    activated = jax.nn.gelu(hidden).astype(jnp.bfloat16)
    projected = jnp.dot(activated, down_weight, preferred_element_type=jnp.float32)
    block_out = stem_grid.reshape(-1, WIDTH) + layer_scale * projected
    pooled = lax.optimization_barrier(jnp.mean(block_out.reshape(tile_total, half_tile, 2, half_tile, 2, WIDTH), axis=(2, 4)))
    pooled = pooled.reshape(tile_total, half_tile * half_tile, WIDTH)
    stored = (patches, padded, centred, inv_std, normed, hidden, activated, projected)
    return (pooled, stored)

def backward_head(stored, cotangent, down_weight, layer_scale):
    patches, padded, centred, inv_std, normed, hidden, activated, projected = stored
    tile_total = cotangent.shape[0]
    half_tile = TILE // 2
    spread_out = jnp.broadcast_to(cotangent.reshape(tile_total, half_tile, 1, half_tile, 1, WIDTH), (tile_total, half_tile, 2, half_tile, 2, WIDTH))
    grad_block = (0.25 * spread_out).reshape(-1, WIDTH)
    scale_term = lax.optimization_barrier(jnp.sum(grad_block * projected, axis=0))
    grad_proj = (grad_block * layer_scale).astype(jnp.bfloat16)
    down_term = lax.dot_general(activated, grad_proj, (((0,), (0,)), ((), ())), preferred_element_type=jnp.float32)
    grad_act = lax.dot_general(grad_proj, down_weight, (((1,), (1,)), ((), ())), preferred_element_type=jnp.float32)
    grad_hidden = jax.vjp(jax.nn.gelu, hidden)[1](grad_act)[0].astype(jnp.bfloat16)
    return (scale_term, down_term, grad_hidden, grad_block)

def backward_middle(stored, grad_hidden, up_weight, norm_gain):
    patches, padded, centred, inv_std, normed, hidden, activated, projected = stored
    up_term = lax.dot_general(normed, grad_hidden, (((0,), (0,)), ((), ())), preferred_element_type=jnp.float32)
    grad_normed = lax.dot_general(grad_hidden, up_weight, (((1,), (1,)), ((), ())), preferred_element_type=jnp.float32)
    gain_term = lax.optimization_barrier(jnp.sum(grad_normed * centred, axis=0))
    scaled = grad_normed * norm_gain
    grad_mixed = inv_std * (scaled - lax.optimization_barrier(jnp.mean(scaled, axis=1, keepdims=True)) - centred * lax.optimization_barrier(jnp.mean(scaled * centred, axis=1, keepdims=True)))
    return (gain_term, up_term, grad_mixed)

def backward_tail(stored, grad_mixed, grad_block, depth_weight):
    patches, padded, centred, inv_std, normed, hidden, activated, projected = stored
    tile_total = padded.shape[0]
    reach = KERNEL // 2
    grid_grad = grad_mixed.reshape(tile_total, TILE, TILE, WIDTH)
    grad_padded = jnp.pad(grid_grad, ((0, 0), (reach, reach), (reach, reach), (0, 0)))
    kernel = depth_weight.astype(jnp.float32)
    depth_rows = []
    inner = jnp.zeros_like(grid_grad)
    for row_tap in range(KERNEL):
        for col_tap in range(KERNEL):
            window = padded[:, row_tap:row_tap + TILE, col_tap:col_tap + TILE, :]
            depth_rows.append(lax.optimization_barrier(jnp.sum(window * grid_grad, axis=(0, 1, 2))))
            row_start = KERNEL - 1 - row_tap
            col_start = KERNEL - 1 - col_tap
            inner = inner + grad_padded[:, row_start:row_start + TILE, col_start:col_start + TILE, :] * kernel[row_tap * KERNEL + col_tap]
    depth_term = jnp.stack(depth_rows)
    grad_stem = (grad_block + inner.reshape(-1, WIDTH)).astype(jnp.bfloat16)
    stem_term = lax.dot_general(patches, grad_stem, (((0,), (0,)), ((), ())), preferred_element_type=jnp.float32)
    return (depth_term, stem_term)

def reference(pixels, tile_counts, text_gaps, stem_weight, depth_weight, norm_gain, up_weight, down_weight, layer_scale, embed_grad):
    owner_span = tile_counts * FEAT_TILE + text_gaps
    offsets = (jnp.cumsum(owner_span, axis=0) - owner_span + text_gaps).astype(jnp.int32)
    prefix = (jnp.cumsum(tile_counts, axis=1) - tile_counts).astype(jnp.int32)
    prefix_end = (prefix + tile_counts).astype(jnp.int32)
    tile_rank = jnp.arange(N_ENC * MEAN_TILES, dtype=jnp.int32)
    owner_index = lax.optimization_barrier(jnp.sum((prefix_end[:, None, :] <= tile_rank[None, :, None]).astype(jnp.int32), axis=2)).astype(jnp.int32)
    slot_index = (tile_rank[None, :] - jnp.take_along_axis(prefix, owner_index, axis=1)).astype(jnp.int32)
    source = (owner_index * SLOTS + slot_index).astype(jnp.int32)
    base_pos = jnp.take_along_axis(offsets, owner_index, axis=1) + slot_index * FEAT_TILE
    positions = (base_pos[:, :, None] + jnp.arange(FEAT_TILE, dtype=jnp.int32)[None, None, :]).astype(jnp.int32)

    def one_row(row_args):
        row_pixels, row_source, row_owner, row_positions = row_args
        tile_block = jnp.take(row_pixels, row_source, axis=0)
        pooled, stored = encode(tile_block, stem_weight, depth_weight, norm_gain, up_weight, down_weight, layer_scale)
        cotangent = embed_grad[row_owner[:, None], row_positions].astype(jnp.float32)
        scale_term, down_term, grad_hidden, grad_block = backward_head(stored, cotangent, down_weight, layer_scale)
        gain_term, up_term, grad_mixed = backward_middle(stored, grad_hidden, up_weight, norm_gain)
        depth_term, stem_term = backward_tail(stored, grad_mixed, grad_block, depth_weight)
        return (pooled.astype(jnp.bfloat16), (stem_term, depth_term, gain_term, up_term, down_term, scale_term))
    features, terms = lax.map(one_row, (pixels, source, owner_index, positions))
    owner_grid = jnp.broadcast_to(owner_index[:, :, None], positions.shape)
    image_embeds = jnp.zeros((N_ENC, SEQ, WIDTH), jnp.bfloat16).at[owner_grid, positions].set(features)
    grad_scale = 1.0 / math.sqrt(N_DEC * N_ENC * MEAN_TILES * FEAT_TILE)
    stem_grad = lax.optimization_barrier(jnp.sum(terms[0], axis=0)) * grad_scale
    depth_grad = lax.optimization_barrier(jnp.sum(terms[1], axis=0)) * grad_scale
    gain_grad = lax.optimization_barrier(jnp.sum(terms[2], axis=0)) * grad_scale
    up_grad = lax.optimization_barrier(jnp.sum(terms[3], axis=0)) * grad_scale
    down_grad = lax.optimization_barrier(jnp.sum(terms[4], axis=0)) * grad_scale
    scale_grad = lax.optimization_barrier(jnp.sum(terms[5], axis=0)) * grad_scale
    return (image_embeds, stem_grad, depth_grad, gain_grad, up_grad, down_grad, scale_grad)
```

```python
import math

import jax
import jax.numpy as jnp
from jax import lax
from jax.sharding import Mesh
from jax.sharding import PartitionSpec as P

WIDTH = 384
KERNEL = 7
PATCH_CH = 48
TILE = 8
MEAN_TILES = 3
SLOTS = 9
FEAT_TILE = 16
LANES = 128
PACK_ROWS = 5120
DEC = ("y", "core")
ENC = ("x", "zh", "zl")
PLANE = ("x", "y")


epsilon = 1e-06


def encode(tile_block, stem_weight, depth_weight, norm_gain, up_weight, down_weight, layer_scale):
    tile_total = tile_block.shape[0]
    reach = KERNEL // 2
    half_tile = TILE // 2
    patches = tile_block.reshape(tile_total * TILE * TILE, PATCH_CH)
    stem_out = jnp.dot(patches, stem_weight, preferred_element_type=jnp.float32).astype(
        jnp.bfloat16
    )
    stem_grid = stem_out.reshape(tile_total, TILE, TILE, WIDTH).astype(jnp.float32)
    padded = jnp.pad(stem_grid, ((0, 0), (reach, reach), (reach, reach), (0, 0)))
    kernel = depth_weight.astype(jnp.float32)
    mixed_field = jnp.zeros_like(stem_grid)
    for row_tap in range(KERNEL):
        for col_tap in range(KERNEL):
            mixed_field = (
                mixed_field
                + padded[:, row_tap : row_tap + TILE, col_tap : col_tap + TILE, :]
                * kernel[row_tap * KERNEL + col_tap]
            )
    flat_rows = mixed_field.reshape(-1, WIDTH)
    channel_mean = jnp.mean(flat_rows, axis=1, keepdims=True)
    deviation = flat_rows - channel_mean
    variance = jnp.mean(deviation * deviation, axis=1, keepdims=True)
    inv_std = lax.rsqrt(variance + epsilon)
    centred = deviation * inv_std
    normed = (centred * norm_gain).astype(jnp.bfloat16)
    hidden = jnp.dot(normed, up_weight, preferred_element_type=jnp.float32)
    activated = jax.nn.gelu(hidden).astype(jnp.bfloat16)
    projected = jnp.dot(activated, down_weight, preferred_element_type=jnp.float32)
    block_out = stem_grid.reshape(-1, WIDTH) + layer_scale * projected
    pooled = jnp.mean(block_out.reshape(tile_total, half_tile, 2, half_tile, 2, WIDTH), axis=(2, 4))
    pooled = pooled.reshape(tile_total, half_tile * half_tile, WIDTH)
    stored = (patches, padded, centred, inv_std, normed, hidden, activated, projected)
    return (pooled, stored)


def backward_head(stored, cotangent, down_weight, layer_scale):
    patches, padded, centred, inv_std, normed, hidden, activated, projected = stored
    tile_total = cotangent.shape[0]
    half_tile = TILE // 2
    spread_out = jnp.broadcast_to(
        cotangent.reshape(tile_total, half_tile, 1, half_tile, 1, WIDTH),
        (tile_total, half_tile, 2, half_tile, 2, WIDTH),
    )
    grad_block = (0.25 * spread_out).reshape(-1, WIDTH)
    scale_term = jnp.sum(grad_block * projected, axis=0)
    grad_proj = (grad_block * layer_scale).astype(jnp.bfloat16)
    down_term = lax.dot_general(
        activated, grad_proj, (((0,), (0,)), ((), ())), preferred_element_type=jnp.float32
    )
    grad_act = lax.dot_general(
        grad_proj, down_weight, (((1,), (1,)), ((), ())), preferred_element_type=jnp.float32
    )
    grad_hidden = jax.vjp(jax.nn.gelu, hidden)[1](grad_act)[0].astype(jnp.bfloat16)
    return (scale_term, down_term, grad_hidden, grad_block)


def backward_middle(stored, grad_hidden, up_weight, norm_gain):
    patches, padded, centred, inv_std, normed, hidden, activated, projected = stored
    up_term = lax.dot_general(
        normed, grad_hidden, (((0,), (0,)), ((), ())), preferred_element_type=jnp.float32
    )
    grad_normed = lax.dot_general(
        grad_hidden, up_weight, (((1,), (1,)), ((), ())), preferred_element_type=jnp.float32
    )
    gain_term = jnp.sum(grad_normed * centred, axis=0)
    scaled = grad_normed * norm_gain
    grad_mixed = inv_std * (
        scaled
        - jnp.mean(scaled, axis=1, keepdims=True)
        - centred * jnp.mean(scaled * centred, axis=1, keepdims=True)
    )
    return (gain_term, up_term, grad_mixed)


def backward_tail(stored, grad_mixed, grad_block, depth_weight):
    patches, padded, centred, inv_std, normed, hidden, activated, projected = stored
    tile_total = padded.shape[0]
    reach = KERNEL // 2
    grid_grad = grad_mixed.reshape(tile_total, TILE, TILE, WIDTH)
    grad_padded = jnp.pad(grid_grad, ((0, 0), (reach, reach), (reach, reach), (0, 0)))
    kernel = depth_weight.astype(jnp.float32)
    depth_rows = []
    inner = jnp.zeros_like(grid_grad)
    for row_tap in range(KERNEL):
        for col_tap in range(KERNEL):
            window = padded[:, row_tap : row_tap + TILE, col_tap : col_tap + TILE, :]
            depth_rows.append(jnp.sum(window * grid_grad, axis=(0, 1, 2)))
            row_start = KERNEL - 1 - row_tap
            col_start = KERNEL - 1 - col_tap
            inner = (
                inner
                + grad_padded[:, row_start : row_start + TILE, col_start : col_start + TILE, :]
                * kernel[row_tap * KERNEL + col_tap]
            )
    depth_term = jnp.stack(depth_rows)
    grad_stem = (grad_block + inner.reshape(-1, WIDTH)).astype(jnp.bfloat16)
    stem_term = lax.dot_general(
        patches, grad_stem, (((0,), (0,)), ((), ())), preferred_element_type=jnp.float32
    )
    return (depth_term, stem_term)


def pack(terms):
    rows = [term.reshape(-1, LANES) for term in terms]
    used = sum(part.shape[0] for part in rows)
    rows.append(jnp.zeros((PACK_ROWS - used, LANES), jnp.float32))
    return jnp.concatenate(rows).astype(jnp.bfloat16)


def unpack(packed, like, scale):
    out, at = [], 0
    for term in like:
        count = term.size // LANES
        piece = packed[at : at + count].astype(jnp.float32) * scale
        out.append(piece.reshape(term.shape))
        at += count
    return out


def swap_blocks(blocks, axes):
    return lax.all_to_all(blocks, axes, 0, 0, tiled=True)


def sum_blocks(blocks):
    return jnp.sum(blocks.astype(jnp.float32), axis=0).astype(jnp.bfloat16)


def spread(block, copies):
    return jnp.broadcast_to(block[None], (copies,) + block.shape)


def sum_all(packed):
    half = sum_blocks(swap_blocks(packed.reshape(2, PACK_ROWS // 2, LANES), "core"))
    part = sum_blocks(swap_blocks(half.reshape(16, PACK_ROWS // 32, LANES), PLANE))
    part = sum_blocks(swap_blocks(spread(part, 4), "zl"))
    part = sum_blocks(swap_blocks(spread(part, 4), "zh"))
    half = swap_blocks(spread(part, 16), PLANE).reshape(PACK_ROWS // 2, LANES)
    return swap_blocks(spread(half, 2), "core").reshape(PACK_ROWS, LANES)


def on_device(
    pixels,
    tile_counts,
    text_gaps,
    stem_weight,
    depth_weight,
    norm_gain,
    up_weight,
    down_weight,
    layer_scale,
    embed_grad,
):
    n_enc = 64
    n_dec = lax.axis_size(DEC)
    dec_here = lax.axis_index(DEC)
    count_here = tile_counts[0, 0]
    block_rows = SLOTS * FEAT_TILE
    seq_rows = embed_grad.shape[1]
    weights = (stem_weight, depth_weight, norm_gain, up_weight, down_weight, layer_scale)
    column = lax.all_gather(
        jnp.concatenate([tile_counts[0], text_gaps[0]])[None, :], DEC, axis=0, tiled=True
    )
    col_counts = column[:, 0]
    col_gaps = column[:, 1]
    owner_span = col_counts * FEAT_TILE + col_gaps
    offsets = jnp.cumsum(owner_span) - owner_span + col_gaps
    dec_ids = jnp.arange(n_dec)
    own_offset = jnp.sum(jnp.where(dec_ids == dec_here, offsets, 0))
    occupied = jnp.arange(SLOTS) < count_here
    gathered = lax.all_gather(embed_grad[0], DEC, axis=0, tiled=True)
    pooled, stored = encode(pixels[0], *weights)
    owner_block = jnp.where(occupied[:, None, None], pooled, 0.0).astype(jnp.bfloat16)
    placed = lax.dynamic_update_slice(
        jnp.zeros((n_dec * seq_rows, WIDTH), jnp.bfloat16),
        owner_block.reshape(block_rows, WIDTH),
        (own_offset, 0),
    )
    sequence = lax.psum_scatter(placed, DEC, scatter_dimension=0, tiled=True)
    taken_rows = lax.dynamic_slice(gathered, (own_offset, 0), (block_rows, WIDTH))
    own_grad = jnp.where(
        occupied[:, None, None], taken_rows.reshape(SLOTS, FEAT_TILE, WIDTH), jnp.bfloat16(0)
    )
    cotangent = own_grad.astype(jnp.float32)
    scale_term, down_term, grad_hidden, grad_block = backward_head(
        stored, cotangent, down_weight, layer_scale
    )
    gain_term, up_term, grad_mixed = backward_middle(stored, grad_hidden, up_weight, norm_gain)
    depth_term, stem_term = backward_tail(stored, grad_mixed, grad_block, depth_weight)
    terms = (stem_term, depth_term, gain_term, up_term, down_term, scale_term)
    grad_scale = 1.0 / math.sqrt(n_dec * n_enc * MEAN_TILES * FEAT_TILE)
    return (sequence[None], *unpack(sum_all(pack(terms)), terms, grad_scale))


def solution(mesh):
    fine = Mesh(mesh.devices.reshape(4, 4, 4, 4, 2), ("x", "zh", "zl", "y", "core"))
    return jax.shard_map(
        on_device,
        mesh=fine,
        in_specs=(
            P(DEC, ENC, None),
            P(DEC, ENC),
            P(DEC, ENC),
            P(),
            P(),
            P(),
            P(),
            P(),
            P(),
            P(ENC, DEC, None),
        ),
        out_specs=(P(ENC, DEC, None), P(), P(), P(), P(), P(), P()),
        check_vma=False,
    )
```

```python
import math

import jax
import jax.numpy as jnp
from jax import lax
from jax.experimental import pallas as pl
from jax.experimental.pallas import tpu as pltpu
from jax.sharding import Mesh
from jax.sharding import PartitionSpec as P

WIDTH = 384
INNER = 768
KERNEL = 7
REACH = KERNEL // 2
PATCH_CH = 48
TILE = 8
MEAN_TILES = 3
SLOTS = 9
FEAT_TILE = 16
N_OWNERS = 512
N_DEC = 8
SHARD = 208
SEQ = N_DEC * SHARD
POSITIONS = SLOTS * TILE * TILE
BLOCK_ROWS = SLOTS * FEAT_TILE
LANES = 128
CHUNKS = WIDTH // LANES
UP_AT = 0
DOWN_AT = UP_AT + (INNER // LANES) * WIDTH
STEM_AT = DOWN_AT + CHUNKS * INNER
SMALL_AT = STEM_AT + CHUNKS * PATCH_CH
SMALL_ROWS = 64
PACK_USED = SMALL_AT + CHUNKS * SMALL_ROWS
PACK_ROWS = 5120
HALF_ROWS = PACK_ROWS // 2
DEC = ("y", "core")
ENC = ("x", "zh", "zl")
PLANE = ("x", "y")
VMEM_BYTES = 50 * 1024 * 1024

epsilon = 1e-06
GELU_A = math.sqrt(2.0 / math.pi)
GELU_B = 0.044715
bf16 = jnp.bfloat16
f32 = jnp.float32


def lanes(chunk):
    return slice(chunk * LANES, (chunk + 1) * LANES)


def column_shift(rows, step):
    if step == 0:
        return rows
    column = lax.broadcasted_iota(jnp.int32, (TILE, LANES), 0) + step
    inside = (column >= 0) & (column < TILE)
    return [jnp.where(inside, pltpu.roll(row, (-step) % TILE, 0), 0.0) for row in rows]


def depthwise(rows, kernel_ref, chunk, sign):
    out = [jnp.zeros((TILE, LANES), f32)] * TILE
    for col_tap in range(KERNEL):
        moved = column_shift(rows, sign * (col_tap - REACH))
        for row_tap in range(KERNEL):
            tap = row_tap * KERNEL + col_tap
            weight = jnp.broadcast_to(kernel_ref[tap : tap + 1, lanes(chunk)], (TILE, LANES))
            for i in range(TILE):
                source = i + sign * (row_tap - REACH)
                if 0 <= source < TILE:
                    out[i] = out[i] + moved[source] * weight
    return out


def forward_kernel(
    count_ref, patches_ref, stem_w_ref, depth_w_ref, gain_ref, up_ref, down_ref, layer_ref,
    stem_ref, centred_ref, inv_ref, hidden_ref, projected_ref, feat_ref,
    taps_ref, field_ref, mixed_ref, normed_ref, act_ref, pool_ref,
):
    taps_ref[...] = depth_w_ref[...].astype(f32)
    stem = jnp.dot(patches_ref[...], stem_w_ref[...], preferred_element_type=f32).astype(bf16)
    stem_ref[...] = stem
    field_ref[...] = stem.astype(f32).reshape(SLOTS * TILE, TILE, WIDTH)
    gain = gain_ref[...]

    def mix(t, carry):
        first = t * TILE
        for chunk in range(CHUNKS):
            rows = [field_ref[first + i, :, lanes(chunk)] for i in range(TILE)]
            out = depthwise(rows, taps_ref, chunk, 1)
            for i in range(TILE):
                mixed_ref[i, :, lanes(chunk)] = out[i]
        for i in range(0, TILE, 2):
            row = mixed_ref[i : i + 2].reshape(2 * TILE, WIDTH)
            deviation = row - jnp.mean(row, axis=1, keepdims=True)
            inv_std = lax.rsqrt(jnp.mean(deviation * deviation, axis=1, keepdims=True) + epsilon)
            centred = deviation * inv_std
            at = pl.ds(pl.multiple_of((first + i) * TILE, 2 * TILE), 2 * TILE)
            centred_ref[at, :] = centred
            inv_ref[at, :] = jnp.broadcast_to(inv_std, (2 * TILE, LANES))
            normed_ref[at, :] = (centred * gain).astype(bf16)
        return carry

    lax.fori_loop(0, SLOTS, mix, 0)
    normed = normed_ref[...]
    for n in range(0, INNER, 256):
        hidden_ref[:, n : n + 256] = jnp.dot(
            normed, up_ref[:, n : n + 256], preferred_element_type=f32
        )

    def activate(r, carry):
        at = pl.ds(pl.multiple_of(r * 16, 16), 16)
        v = hidden_ref[at, :]
        t = jnp.tanh(GELU_A * (v + GELU_B * (v * v * v)))
        act_ref[at, :] = (0.5 * v * (1.0 + t)).astype(bf16)
        return carry

    lax.fori_loop(0, POSITIONS // 16, activate, 0)
    projected_ref[...] = jnp.dot(act_ref[...], down_ref[...], preferred_element_type=f32)
    layer = layer_ref[...]
    count = count_ref[0]

    def pool(t, carry):
        keep = jnp.where(t < count, 0.25, 0.0).astype(f32)
        for pair in range(TILE // 2):
            total = None
            for half in range(2):
                i = t * TILE + 2 * pair + half
                at = pl.ds(pl.multiple_of(i * TILE, TILE), TILE)
                block = field_ref[i] + layer * projected_ref[at, :]
                total = block if total is None else total + block
            total = (total + pltpu.roll(total, TILE - 1, 0)) * keep
            for chunk in range(CHUNKS):
                pool_ref[chunk, pair * TILE : (pair + 1) * TILE, :] = total[:, lanes(chunk)]
        at = pl.ds(pl.multiple_of(t * FEAT_TILE, FEAT_TILE), FEAT_TILE)
        for chunk in range(CHUNKS):
            pooled = pool_ref[chunk, pl.ds(0, FEAT_TILE, stride=2), :].astype(bf16)
            for d in range(N_DEC):
                feat_ref[d, at, lanes(chunk)] = pooled
        return carry

    lax.fori_loop(0, SLOTS, pool, 0)


def forward(count, patches, stem_w, depth_w, gain, up, down, layer):
    vmem = pl.BlockSpec(memory_space=pltpu.VMEM)
    shapes = (
        ((POSITIONS, WIDTH), bf16),
        ((POSITIONS, WIDTH), f32),
        ((POSITIONS, LANES), f32),
        ((POSITIONS, INNER), f32),
        ((POSITIONS, WIDTH), f32),
        ((N_DEC, BLOCK_ROWS, WIDTH), bf16),
    )
    return pl.pallas_call(
        forward_kernel,
        out_shape=[jax.ShapeDtypeStruct(*shape) for shape in shapes],
        in_specs=[pl.BlockSpec(memory_space=pltpu.SMEM)] + [vmem] * 7,
        out_specs=[vmem] * 6,
        scratch_shapes=[
            pltpu.VMEM((KERNEL * KERNEL, WIDTH), f32),
            pltpu.VMEM((SLOTS * TILE, TILE, WIDTH), f32),
            pltpu.VMEM((TILE, TILE, WIDTH), f32),
            pltpu.VMEM((POSITIONS, WIDTH), bf16),
            pltpu.VMEM((POSITIONS, INNER), bf16),
            pltpu.VMEM((CHUNKS, TILE // 2 * TILE, LANES), f32),
        ],
        compiler_params=pltpu.CompilerParams(vmem_limit_bytes=VMEM_BYTES),
        cost_estimate=pl.CostEstimate(
            flops=4 * POSITIONS * WIDTH * INNER, bytes_accessed=8 << 20, transcendentals=0
        ),
        name="block_forward",
    )(count, patches, stem_w, depth_w, gain, up, down, layer)


def rows_times_rows(a, b):
    return lax.dot_general(a, b, (((1,), (1,)), ((), ())), preferred_element_type=f32)


def over_positions(a, b):
    return lax.dot_general(a, b, (((0,), (0,)), ((), ())), preferred_element_type=f32)


def backward_kernel(
    place_ref, count_ref, own_ref, other_ref, patches_ref, stem_ref, centred_ref, inv_ref,
    hidden_ref, projected_ref, depth_w_ref, gain_ref, up_ref, down_ref, layer_ref,
    packed_ref, spans_ref,
    taps_ref, embed_ref, block_ref, proj_ref, act_ref, work_ref, ghid_ref, normed_ref,
    mixed_ref, gstem_ref, taps_sum_ref, rows_sum_ref,
):
    y_here, core_here = place_ref[0], place_ref[1]
    dec_here = 2 * y_here + core_here
    taps_ref[...] = depth_w_ref[...].astype(f32)
    counts, gaps = [None] * N_DEC, [None] * N_DEC
    for y in range(N_DEC // 2):
        embed_ref[pl.ds(pl.multiple_of((2 * y + core_here) * SHARD, 16), SHARD), :] = own_ref[y, :SHARD, :]
        embed_ref[pl.ds(pl.multiple_of((2 * y + 1 - core_here) * SHARD, 16), SHARD), :] = other_ref[y, :SHARD, :]
        mine = own_ref[y, SHARD:, :LANES].astype(f32)
        theirs = other_ref[y, SHARD:, :LANES].astype(f32)
        for core in range(2):
            tail = jnp.where(core_here == core, mine, theirs)
            counts[2 * y + core] = tail[0, 0].astype(jnp.int32)
            gaps[2 * y + core] = tail[0, 1].astype(jnp.int32)
    embed_ref[SEQ:, :] = jnp.zeros((16, WIDTH), bf16)
    at, own_offset = jnp.int32(0), jnp.int32(0)
    for d in range(N_DEC):
        start = at + gaps[d]
        spans_ref[d] = start
        spans_ref[N_DEC + d] = counts[d]
        own_offset = jnp.where(dec_here == d, start, own_offset)
        at = start + FEAT_TILE * counts[d]
    count = count_ref[0]
    layer = layer_ref[...]
    gain = gain_ref[...]
    rows_sum_ref[...] = jnp.zeros((2, TILE, WIDTH), f32)
    taps_sum_ref[...] = jnp.zeros((KERNEL * KERNEL, TILE, WIDTH), f32)

    def spread_tile(t, carry):
        start = own_offset + FEAT_TILE * t
        base = lax.div(start, 16)
        row = lax.broadcasted_iota(jnp.int32, (64, 32), 0)
        col = lax.broadcasted_iota(jnp.int32, (64, 32), 1)
        feat = lax.shift_right_logical(row, 4) * 4 + (lax.shift_right_logical(row, 1) & 3)
        hit = (col == feat + (start - 16 * base)) & (t < count)
        pick = jnp.where(hit, 0.25, 0.0).astype(bf16)
        window = embed_ref[pl.ds(pl.multiple_of(base * 16, 16), 32), :]
        block = jnp.dot(pick, window, preferred_element_type=f32)
        at = pl.ds(pl.multiple_of(t * 64, 64), 64)
        block_ref[at, :] = block
        proj_ref[at, :] = (block * layer).astype(bf16)
        product = block * projected_ref[at, :]
        rows_sum_ref[0] += jnp.sum(product.reshape(TILE, TILE, WIDTH), axis=0)
        normed_ref[at, :] = (centred_ref[at, :] * gain).astype(bf16)
        return carry

    lax.fori_loop(0, SLOTS, spread_tile, 0)
    proj = proj_ref[...]
    for n in range(0, INNER, 256):
        work_ref[:, n : n + 256] = rows_times_rows(proj, down_ref[n : n + 256, :])

    def activate(r, carry):
        at = pl.ds(pl.multiple_of(r * 16, 16), 16)
        v = hidden_ref[at, :]
        square = v * v
        t = jnp.tanh(GELU_A * (v + GELU_B * (square * v)))
        half = 0.5 * (1.0 + t)
        act_ref[at, :] = (v * half).astype(bf16)
        slope = half + (0.5 * GELU_A) * v * (1.0 - t * t) * (1.0 + (3.0 * GELU_B) * square)
        ghid_ref[at, :] = (work_ref[at, :] * slope).astype(bf16)
        return carry

    lax.fori_loop(0, POSITIONS // 16, activate, 0)
    for n in range(0, INNER, 256):
        term = over_positions(act_ref[:, n : n + 256], proj).astype(bf16)
        for chunk in range(CHUNKS):
            to = DOWN_AT + chunk * INNER + n
            packed_ref[to : to + 256, :] = term[:, lanes(chunk)]
    normed = normed_ref[...]
    for n in range(0, INNER, 256):
        term = over_positions(normed, ghid_ref[:, n : n + 256]).astype(bf16)
        for k in range(2):
            to = UP_AT + (n // LANES + k) * WIDTH
            packed_ref[to : to + WIDTH, :] = term[:, lanes(k)]
    work_ref[:, :WIDTH] = rows_times_rows(ghid_ref[...], up_ref[...])

    def unmix(t, carry):
        gain_sum = jnp.zeros((TILE, WIDTH), f32)
        for i in range(0, TILE, 2):
            at = pl.ds(pl.multiple_of((t * TILE + i) * TILE, 2 * TILE), 2 * TILE)
            grad = work_ref[at, :WIDTH]
            centred = centred_ref[at, :]
            gain_sum += jnp.sum((grad * centred).reshape(2, TILE, WIDTH), axis=0)
            scaled = grad * gain
            mean = jnp.mean(scaled, axis=1, keepdims=True)
            mean_c = jnp.mean(scaled * centred, axis=1, keepdims=True)
            mixed = (scaled - mean - centred * mean_c) * inv_ref[at, :1]
            mixed_ref[i : i + 2] = mixed.reshape(2, TILE, WIDTH)
        rows_sum_ref[1] += gain_sum
        for chunk in range(CHUNKS):
            grads = [mixed_ref[i, :, lanes(chunk)] for i in range(TILE)]
            stem = []
            for i in range(0, TILE, 2):
                at = pl.ds(pl.multiple_of((t * TILE + i) * TILE, 2 * TILE), 2 * TILE)
                pair = stem_ref[at, lanes(chunk)].astype(f32)
                stem += [pair[:TILE], pair[TILE:]]
            for col_tap in range(KERNEL):
                moved = column_shift(stem, col_tap - REACH)
                for row_tap in range(KERNEL):
                    total = None
                    for i in range(TILE):
                        source = i + row_tap - REACH
                        if 0 <= source < TILE:
                            part = moved[source] * grads[i]
                            total = part if total is None else total + part
                    taps_sum_ref[row_tap * KERNEL + col_tap, :, lanes(chunk)] += total
            inner = depthwise(grads, taps_ref, chunk, -1)
            for i in range(0, TILE, 2):
                at = pl.ds(pl.multiple_of((t * TILE + i) * TILE, 2 * TILE), 2 * TILE)
                block = block_ref[at, lanes(chunk)]
                pair = jnp.concatenate([inner[i], inner[i + 1]], axis=0)
                gstem_ref[at, lanes(chunk)] = (block + pair).astype(bf16)
        return carry

    lax.fori_loop(0, SLOTS, unmix, 0)
    stem_term = over_positions(patches_ref[...], gstem_ref[...]).astype(bf16)
    small = jnp.concatenate(
        [
            jnp.sum(taps_sum_ref[...], axis=1),
            jnp.sum(rows_sum_ref[...], axis=1),
            jnp.zeros((SMALL_ROWS - KERNEL * KERNEL - 2, WIDTH), f32),
        ],
        axis=0,
    ).astype(bf16)
    for chunk in range(CHUNKS):
        to = STEM_AT + chunk * PATCH_CH
        packed_ref[to : to + PATCH_CH, :] = stem_term[:, lanes(chunk)]
        to = SMALL_AT + chunk * SMALL_ROWS
        packed_ref[to : to + SMALL_ROWS, :] = small[:, lanes(chunk)]
    packed_ref[PACK_USED:, :] = jnp.zeros((PACK_ROWS - PACK_USED, LANES), bf16)


def backward(place, count, own, other, patches, stored, depth_w, gain, up, down, layer):
    vmem = pl.BlockSpec(memory_space=pltpu.VMEM)
    smem = pl.BlockSpec(memory_space=pltpu.SMEM)
    return pl.pallas_call(
        backward_kernel,
        out_shape=[
            jax.ShapeDtypeStruct((PACK_ROWS, LANES), bf16),
            jax.ShapeDtypeStruct((2 * N_DEC,), jnp.int32),
        ],
        in_specs=[smem, smem] + [vmem] * 13,
        out_specs=[vmem, smem],
        scratch_shapes=[
            pltpu.VMEM((KERNEL * KERNEL, WIDTH), f32),
            pltpu.VMEM((SEQ + 16, WIDTH), bf16),
            pltpu.VMEM((POSITIONS, WIDTH), f32),
            pltpu.VMEM((POSITIONS, WIDTH), bf16),
            pltpu.VMEM((POSITIONS, INNER), bf16),
            pltpu.VMEM((POSITIONS, INNER), f32),
            pltpu.VMEM((POSITIONS, INNER), bf16),
            pltpu.VMEM((POSITIONS, WIDTH), bf16),
            pltpu.VMEM((TILE, TILE, WIDTH), f32),
            pltpu.VMEM((POSITIONS, WIDTH), bf16),
            pltpu.VMEM((KERNEL * KERNEL, TILE, WIDTH), f32),
            pltpu.VMEM((2, TILE, WIDTH), f32),
        ],
        compiler_params=pltpu.CompilerParams(vmem_limit_bytes=VMEM_BYTES),
        cost_estimate=pl.CostEstimate(
            flops=8 * POSITIONS * WIDTH * INNER, bytes_accessed=10 << 20, transcendentals=0
        ),
        name="block_backward",
    )(place, count, own, other, patches, *stored, depth_w, gain, up, down, layer)


def place_kernel(place_ref, spans_ref, feat_ref, out_ref, rows_ref):
    base = (2 * place_ref[0] + place_ref[1]) * SHARD
    rows_ref[...] = jnp.zeros((FEAT_TILE + SHARD + FEAT_TILE, WIDTH), f32)

    def one(k, carry):
        d = lax.div(k, SLOTS)
        j = k - d * SLOTS
        to = spans_ref[d] + FEAT_TILE * j - base

        @pl.when((j < spans_ref[N_DEC + d]) & (to > -FEAT_TILE) & (to < SHARD))
        def _():
            at = pl.ds(pl.multiple_of(j * FEAT_TILE, FEAT_TILE), FEAT_TILE)
            chunk = lax.div(to + FEAT_TILE, 16)
            row = lax.broadcasted_iota(jnp.int32, (32, FEAT_TILE), 0)
            col = lax.broadcasted_iota(jnp.int32, (32, FEAT_TILE), 1)
            pick = jnp.where(row == col + (to + FEAT_TILE - 16 * chunk), 1.0, 0.0).astype(bf16)
            window = pl.ds(pl.multiple_of(chunk * 16, 16), 32)
            rows_ref[window, :] += jnp.dot(pick, feat_ref[d, at, :], preferred_element_type=f32)

        return carry

    lax.fori_loop(0, N_DEC * SLOTS, one, 0)
    out_ref[...] = rows_ref[FEAT_TILE : FEAT_TILE + SHARD, :].astype(bf16)


def place_features(place, spans, feat):
    vmem = pl.BlockSpec(memory_space=pltpu.VMEM)
    smem = pl.BlockSpec(memory_space=pltpu.SMEM)
    return pl.pallas_call(
        place_kernel,
        out_shape=jax.ShapeDtypeStruct((SHARD, WIDTH), bf16),
        in_specs=[smem, smem, vmem],
        out_specs=vmem,
        scratch_shapes=[pltpu.VMEM((FEAT_TILE + SHARD + FEAT_TILE, WIDTH), f32)],
        compiler_params=pltpu.CompilerParams(vmem_limit_bytes=VMEM_BYTES),
        name="place_features",
    )(place, spans, feat)


def unpack_kernel(
    place_ref, own_ref, other_ref, stem_ref, depth_ref, gain_ref, up_ref, down_ref, scale_ref, rows_ref
):
    core = place_ref[1]
    factor = 1.0 / math.sqrt(N_OWNERS * MEAN_TILES * FEAT_TILE)
    rows_ref[pl.ds(pl.multiple_of(core * HALF_ROWS, 16), HALF_ROWS), :] = own_ref[...]
    rows_ref[pl.ds(pl.multiple_of((1 - core) * HALF_ROWS, 16), HALF_ROWS), :] = other_ref[...]

    def piece(at, count):
        return rows_ref[at : at + count, :].astype(f32) * factor

    for k in range(INNER // LANES):
        up_ref[:, lanes(k)] = piece(UP_AT + k * WIDTH, WIDTH)
    for chunk in range(CHUNKS):
        down_ref[:, lanes(chunk)] = piece(DOWN_AT + chunk * INNER, INNER)
        stem_ref[:, lanes(chunk)] = piece(STEM_AT + chunk * PATCH_CH, PATCH_CH)
        small = piece(SMALL_AT + chunk * SMALL_ROWS, SMALL_ROWS)
        taps = KERNEL * KERNEL
        depth_ref[:, lanes(chunk)] = small[:taps]
        scale_ref[:, lanes(chunk)] = small[taps : taps + 1]
        gain_ref[:, lanes(chunk)] = small[taps + 1 : taps + 2]


def unpack(place, own, other):
    vmem = pl.BlockSpec(memory_space=pltpu.VMEM)
    smem = pl.BlockSpec(memory_space=pltpu.SMEM)
    shapes = (
        (PATCH_CH, WIDTH),
        (KERNEL * KERNEL, WIDTH),
        (1, WIDTH),
        (WIDTH, INNER),
        (INNER, WIDTH),
        (1, WIDTH),
    )
    return pl.pallas_call(
        unpack_kernel,
        out_shape=[jax.ShapeDtypeStruct(shape, f32) for shape in shapes],
        in_specs=[smem, vmem, vmem],
        out_specs=[vmem] * 6,
        scratch_shapes=[pltpu.VMEM((PACK_ROWS, LANES), bf16)],
        compiler_params=pltpu.CompilerParams(vmem_limit_bytes=VMEM_BYTES),
        name="unpack_terms",
    )(place, own, other)


def swap_blocks(blocks, axes):
    return lax.all_to_all(blocks, axes, 0, 0, tiled=True)


def sum_blocks(blocks):
    return jnp.sum(blocks.astype(f32), axis=0).astype(bf16)


def spread(block, copies):
    return jnp.broadcast_to(block[None], (copies,) + block.shape)


def swap_cores(x):
    return lax.ppermute(x, "core", [(0, 1), (1, 0)])


def sum_all(packed):
    half = sum_blocks(swap_blocks(packed.reshape(2, HALF_ROWS, LANES), "core"))
    part = sum_blocks(swap_blocks(half.reshape(16, PACK_ROWS // 32, LANES), PLANE))
    part = sum_blocks(swap_blocks(spread(part, 4), "zl"))
    part = sum_blocks(swap_blocks(spread(part, 4), "zh"))
    return swap_blocks(spread(part, 16), PLANE).reshape(HALF_ROWS, LANES)


def on_device(
    pixels,
    tile_counts,
    text_gaps,
    stem_weight,
    depth_weight,
    norm_gain,
    up_weight,
    down_weight,
    layer_scale,
    embed_grad,
):
    place = jnp.stack([lax.axis_index("y"), lax.axis_index("core")]).astype(jnp.int32)
    count = tile_counts.reshape(1)
    gain = norm_gain.reshape(1, WIDTH)
    layer = layer_scale.reshape(1, WIDTH)
    patches = pixels.reshape(POSITIONS, PATCH_CH)
    numbers = jnp.concatenate([tile_counts, text_gaps], axis=1).astype(bf16)
    tail = jnp.pad(numbers, ((0, 7), (0, WIDTH - 2)))
    own = swap_blocks(spread(jnp.concatenate([embed_grad[0], tail]), 4), "y")
    *stored, feat = forward(
        count, patches, stem_weight, depth_weight, gain, up_weight, down_weight, layer
    )
    other = swap_cores(own)
    feats = swap_blocks(feat, DEC)
    packed, spans = backward(
        place, count, own, other, patches, stored, depth_weight, gain, up_weight, down_weight, layer
    )
    half = sum_all(packed)
    stem, depth, gain_grad, up, down, scale = unpack(place, half, swap_cores(half))
    sequence = place_features(place, spans, feats)
    return (
        sequence[None],
        stem,
        depth,
        gain_grad.reshape(WIDTH),
        up,
        down,
        scale.reshape(WIDTH),
    )


def solution(mesh):
    fine = Mesh(mesh.devices.reshape(4, 4, 4, 4, 2), ("x", "zh", "zl", "y", "core"))
    return jax.shard_map(
        on_device,
        mesh=fine,
        in_specs=(
            P(DEC, ENC, None),
            P(DEC, ENC),
            P(DEC, ENC),
            P(),
            P(),
            P(),
            P(),
            P(),
            P(),
            P(ENC, DEC, None),
        ),
        out_specs=(P(ENC, DEC, None), P(), P(), P(), P(), P(), P()),
        check_vma=False,
    )
```

```python
import math

import jax
import jax.numpy as jnp
from jax import lax
from jax.experimental import pallas as pl
from jax.experimental.pallas import tpu as pltpu
from jax.sharding import Mesh
from jax.sharding import PartitionSpec as P

WIDTH = 384
INNER = 768
KERNEL = 7
REACH = KERNEL // 2
PATCH_CH = 48
TILE = 8
MEAN_TILES = 3
SLOTS = 9
FEAT_TILE = 16
N_OWNERS = 512
N_DEC = 8
SHARD = 208
SEQ = N_DEC * SHARD
POSITIONS = SLOTS * TILE * TILE
BLOCK_ROWS = SLOTS * FEAT_TILE
LANES = 128
CHUNKS = WIDTH // LANES
UP_AT = 0
DOWN_AT = UP_AT + (INNER // LANES) * WIDTH
STEM_AT = DOWN_AT + CHUNKS * INNER
SMALL_AT = STEM_AT + CHUNKS * PATCH_CH
SMALL_ROWS = 64
PACK_USED = SMALL_AT + CHUNKS * SMALL_ROWS
PACK_ROWS = 5120
HALF_ROWS = PACK_ROWS // 2
DEC = ("y", "core")
ENC = ("x", "zh", "zl")
PLANE = ("x", "y")
VMEM_BYTES = 24 * 1024 * 1024

epsilon = 1e-06
GELU_A = math.sqrt(2.0 / math.pi)
GELU_B = 0.044715
bf16 = jnp.bfloat16
f32 = jnp.float32


def lanes(chunk):
    return slice(chunk * LANES, (chunk + 1) * LANES)


def column_shift(rows, step):
    if step == 0:
        return rows
    column = lax.broadcasted_iota(jnp.int32, (TILE, LANES), 0) + step
    inside = (column >= 0) & (column < TILE)
    return [jnp.where(inside, pltpu.roll(row, (-step) % TILE, 0), 0.0) for row in rows]


def depthwise(rows, kernel_ref, chunk, sign):
    out = [jnp.zeros((TILE, LANES), f32)] * TILE
    for col_tap in range(KERNEL):
        moved = column_shift(rows, sign * (col_tap - REACH))
        for row_tap in range(KERNEL):
            tap = row_tap * KERNEL + col_tap
            weight = jnp.broadcast_to(kernel_ref[tap : tap + 1, lanes(chunk)], (TILE, LANES))
            for i in range(TILE):
                source = i + sign * (row_tap - REACH)
                if 0 <= source < TILE:
                    out[i] = out[i] + moved[source] * weight
    return out


def in_hbm(x):
    return pltpu.with_memory_space_constraint(x, pltpu.HBM)


class Copies:
    def __init__(self, sems):
        self.sems, self.made = sems, []

    def start(self, source, target):
        copy = pltpu.make_async_copy(source, target, self.sems.at[len(self.made)])
        self.made.append(copy)
        copy.start()
        return copy


def forward_kernel(
    count_ref, patches_ref, stem_w_hbm, depth_w_hbm, gain_ref, up_hbm, down_hbm, layer_ref,
    stem_hbm, centred_hbm, inv_hbm, hidden_hbm, feat_hbm,
    stem_w_ref, depth_w_ref, up_ref, down_ref, stem_ref, centred_ref, inv_ref, hidden_ref,
    projected_ref, feat_ref, taps_ref, field_ref, mixed_ref, normed_ref, act_ref, pool_ref, sems,
):
    copies = Copies(sems)
    stem_w_in = copies.start(stem_w_hbm, stem_w_ref)
    depth_w_in = copies.start(depth_w_hbm, depth_w_ref)
    up_in = copies.start(up_hbm, up_ref)
    down_in = copies.start(down_hbm, down_ref)
    outs = []
    stem_w_in.wait()
    stem = jnp.dot(patches_ref[...], stem_w_ref[...], preferred_element_type=f32).astype(bf16)
    stem_ref[...] = stem
    outs.append(copies.start(stem_ref, stem_hbm))
    field_ref[...] = stem.astype(f32).reshape(SLOTS * TILE, TILE, WIDTH)
    depth_w_in.wait()
    taps_ref[...] = depth_w_ref[...].astype(f32)
    gain = gain_ref[...]

    def mix(t, carry):
        first = t * TILE
        for chunk in range(CHUNKS):
            rows = [field_ref[first + i, :, lanes(chunk)] for i in range(TILE)]
            out = depthwise(rows, taps_ref, chunk, 1)
            for i in range(TILE):
                mixed_ref[i, :, lanes(chunk)] = out[i]
        for i in range(0, TILE, 2):
            row = mixed_ref[i : i + 2].reshape(2 * TILE, WIDTH)
            deviation = row - jnp.mean(row, axis=1, keepdims=True)
            inv_std = lax.rsqrt(jnp.mean(deviation * deviation, axis=1, keepdims=True) + epsilon)
            centred = deviation * inv_std
            at = pl.ds(pl.multiple_of((first + i) * TILE, 2 * TILE), 2 * TILE)
            centred_ref[at, :] = centred
            inv_ref[at, :] = jnp.broadcast_to(inv_std, (2 * TILE, LANES))
            normed_ref[at, :] = (centred * gain).astype(bf16)
        return carry

    lax.fori_loop(0, SLOTS, mix, 0, unroll=True)
    outs.append(copies.start(centred_ref, centred_hbm))
    outs.append(copies.start(inv_ref, inv_hbm))
    up_in.wait()
    normed = normed_ref[...]
    for n in range(0, INNER, 256):
        hidden_ref[:, n : n + 256] = jnp.dot(
            normed, up_ref[:, n : n + 256], preferred_element_type=f32
        )
    outs.append(copies.start(hidden_ref, hidden_hbm))

    def activate(r, carry):
        at = pl.ds(pl.multiple_of(r * 16, 16), 16)
        v = hidden_ref[at, :]
        t = jnp.tanh(GELU_A * (v + GELU_B * (v * v * v)))
        act_ref[at, :] = (0.5 * v * (1.0 + t)).astype(bf16)
        return carry

    lax.fori_loop(0, POSITIONS // 16, activate, 0, unroll=4)
    down_in.wait()
    projected_ref[...] = jnp.dot(act_ref[...], down_ref[...], preferred_element_type=f32)
    layer = layer_ref[...]
    count = count_ref[0]

    def pool(t, carry):
        keep = jnp.where(t < count, 0.25, 0.0).astype(f32)
        for pair in range(TILE // 2):
            total = None
            for half in range(2):
                i = t * TILE + 2 * pair + half
                at = pl.ds(pl.multiple_of(i * TILE, TILE), TILE)
                block = field_ref[i] + layer * projected_ref[at, :]
                total = block if total is None else total + block
            total = (total + pltpu.roll(total, TILE - 1, 0)) * keep
            for chunk in range(CHUNKS):
                pool_ref[chunk, pair * TILE : (pair + 1) * TILE, :] = total[:, lanes(chunk)]
        at = pl.ds(pl.multiple_of(t * FEAT_TILE, FEAT_TILE), FEAT_TILE)
        for chunk in range(CHUNKS):
            feat_ref[at, lanes(chunk)] = pool_ref[chunk, pl.ds(0, FEAT_TILE, stride=2), :].astype(bf16)
        return carry

    lax.fori_loop(0, SLOTS, pool, 0)
    for d in range(N_DEC):
        outs.append(copies.start(feat_ref, feat_hbm.at[d]))
    for out in outs:
        out.wait()


def forward(count, patches, stem_w, depth_w, gain, up, down, layer):
    vmem = pl.BlockSpec(memory_space=pltpu.VMEM)
    smem = pl.BlockSpec(memory_space=pltpu.SMEM)
    hbm = pl.BlockSpec(memory_space=pltpu.HBM)
    stored = (
        ((POSITIONS, WIDTH), bf16),
        ((POSITIONS, WIDTH), f32),
        ((POSITIONS, LANES), f32),
        ((POSITIONS, INNER), f32),
    )
    shapes = stored + (((N_DEC, BLOCK_ROWS, WIDTH), bf16),)
    return pl.pallas_call(
        forward_kernel,
        out_shape=[pltpu.HBM(*shape) for shape in shapes],
        in_specs=[smem, vmem, hbm, hbm, vmem, hbm, hbm, vmem],
        out_specs=[hbm] * 5,
        scratch_shapes=[
            pltpu.VMEM((PATCH_CH, WIDTH), bf16),
            pltpu.VMEM((KERNEL * KERNEL, WIDTH), bf16),
            pltpu.VMEM((WIDTH, INNER), bf16),
            pltpu.VMEM((INNER, WIDTH), bf16),
            *[pltpu.VMEM(*shape) for shape in stored],
            pltpu.VMEM((POSITIONS, WIDTH), f32),
            pltpu.VMEM((BLOCK_ROWS, WIDTH), bf16),
            pltpu.VMEM((KERNEL * KERNEL, WIDTH), f32),
            pltpu.VMEM((SLOTS * TILE, TILE, WIDTH), f32),
            pltpu.VMEM((TILE, TILE, WIDTH), f32),
            pltpu.VMEM((POSITIONS, WIDTH), bf16),
            pltpu.VMEM((POSITIONS, INNER), bf16),
            pltpu.VMEM((CHUNKS, TILE // 2 * TILE, LANES), f32),
            pltpu.SemaphoreType.DMA((16,)),
        ],
        compiler_params=pltpu.CompilerParams(vmem_limit_bytes=VMEM_BYTES),
        cost_estimate=pl.CostEstimate(
            flops=4 * POSITIONS * WIDTH * INNER, bytes_accessed=8 << 20, transcendentals=0
        ),
        name="block_forward",
    )(count, patches, in_hbm(stem_w), in_hbm(depth_w), gain, in_hbm(up), in_hbm(down), layer)


def rows_times_rows(a, b):
    return lax.dot_general(a, b, (((1,), (1,)), ((), ())), preferred_element_type=f32)


def over_positions(a, b):
    return lax.dot_general(a, b, (((0,), (0,)), ((), ())), preferred_element_type=f32)


def rows_sum(x):
    return jnp.sum(x.reshape(-1, TILE, WIDTH), axis=0)


def backward_kernel(
    place_ref, count_ref, own_ref, other_ref, patches_ref, stem_hbm, centred_hbm, inv_hbm,
    hidden_hbm, depth_w_hbm, gain_ref, up_hbm, down_hbm, layer_ref,
    packed_hbm, spans_ref,
    stem_ref, centred_ref, inv_ref, hidden_ref, depth_w_ref, up_ref, down_ref, packed_ref,
    taps_ref, embed_ref, block_ref, proj_ref, act_ref, work_ref, ghid_ref, normed_ref,
    mixed_ref, gstem_ref, taps_sum_ref, gain_sum_ref, scale_sum_ref, sems,
):
    copies = Copies(sems)
    down_in = copies.start(down_hbm, down_ref)
    hidden_in = copies.start(hidden_hbm, hidden_ref)
    centred_in = copies.start(centred_hbm, centred_ref)
    up_in = copies.start(up_hbm, up_ref)
    depth_w_in = copies.start(depth_w_hbm, depth_w_ref)
    inv_in = copies.start(inv_hbm, inv_ref)
    stem_in = copies.start(stem_hbm, stem_ref)
    outs = []
    y_here, core_here = place_ref[0], place_ref[1]
    dec_here = 2 * y_here + core_here
    counts, gaps = [None] * N_DEC, [None] * N_DEC
    for y in range(N_DEC // 2):
        embed_ref[pl.ds(pl.multiple_of((2 * y + core_here) * SHARD, 16), SHARD), :] = own_ref[y, :SHARD, :]
        embed_ref[pl.ds(pl.multiple_of((2 * y + 1 - core_here) * SHARD, 16), SHARD), :] = other_ref[y, :SHARD, :]
        mine = own_ref[y, SHARD:, :LANES].astype(f32)
        theirs = other_ref[y, SHARD:, :LANES].astype(f32)
        for core in range(2):
            tail = jnp.where(core_here == core, mine, theirs)
            counts[2 * y + core] = tail[0, 0].astype(jnp.int32)
            gaps[2 * y + core] = tail[0, 1].astype(jnp.int32)
    embed_ref[SEQ:, :] = jnp.zeros((16, WIDTH), bf16)
    at, own_offset = jnp.int32(0), jnp.int32(0)
    for d in range(N_DEC):
        start = at + gaps[d]
        spans_ref[d] = start
        spans_ref[N_DEC + d] = counts[d]
        own_offset = jnp.where(dec_here == d, start, own_offset)
        at = start + FEAT_TILE * counts[d]
    count = count_ref[0]
    layer = layer_ref[...]
    gain = gain_ref[...]
    gain_sum_ref[...] = jnp.zeros((TILE, WIDTH), f32)
    scale_sum_ref[...] = jnp.zeros((TILE, WIDTH), f32)
    taps_sum_ref[...] = jnp.zeros((KERNEL * KERNEL, TILE, WIDTH), f32)

    def spread_tile(t, carry):
        start = own_offset + FEAT_TILE * t
        base = lax.div(start, 16)
        row = lax.broadcasted_iota(jnp.int32, (64, 32), 0)
        col = lax.broadcasted_iota(jnp.int32, (64, 32), 1)
        feat = lax.shift_right_logical(row, 4) * 4 + (lax.shift_right_logical(row, 1) & 3)
        hit = (col == feat + (start - 16 * base)) & (t < count)
        pick = jnp.where(hit, 0.25, 0.0).astype(bf16)
        window = embed_ref[pl.ds(pl.multiple_of(base * 16, 16), 32), :]
        block = jnp.dot(pick, window, preferred_element_type=f32)
        at = pl.ds(pl.multiple_of(t * 64, 64), 64)
        block_ref[at, :] = block
        proj_ref[at, :] = (block * layer).astype(bf16)
        return carry

    lax.fori_loop(0, SLOTS, spread_tile, 0, unroll=True)
    proj = proj_ref[...]
    down_in.wait()
    for n in range(0, INNER, 256):
        work_ref[:, n : n + 256] = rows_times_rows(proj, down_ref[n : n + 256, :])
    hidden_in.wait()

    def activate(r, carry):
        at = pl.ds(pl.multiple_of(r * 16, 16), 16)
        v = hidden_ref[at, :]
        square = v * v
        t = jnp.tanh(GELU_A * (v + GELU_B * (square * v)))
        half = 0.5 * (1.0 + t)
        act_ref[at, :] = (v * half).astype(bf16)
        slope = half + (0.5 * GELU_A) * v * (1.0 - t * t) * (1.0 + (3.0 * GELU_B) * square)
        ghid_ref[at, :] = (work_ref[at, :] * slope).astype(bf16)
        return carry

    lax.fori_loop(0, POSITIONS // 16, activate, 0, unroll=4)
    up_in.wait()
    work_ref[:, :WIDTH] = rows_times_rows(ghid_ref[...], up_ref[...])
    centred_in.wait()
    inv_in.wait()
    stem_in.wait()
    depth_w_in.wait()
    taps_ref[...] = depth_w_ref[...].astype(f32)
    normed_ref[...] = (centred_ref[...] * gain).astype(bf16)

    def down_part(n):
        term = over_positions(act_ref[:, n : n + 256], proj)
        scale_sum_ref[...] += rows_sum(term * down_ref[n : n + 256, :].astype(f32))
        term = term.astype(bf16)
        for chunk in range(CHUNKS):
            to = DOWN_AT + chunk * INNER + n
            packed_ref[to : to + 256, :] = term[:, lanes(chunk)]

    def up_part(n):
        term = over_positions(normed_ref[...], ghid_ref[:, n : n + 256]).astype(bf16)
        for k in range(2):
            to = UP_AT + (n // LANES + k) * WIDTH
            packed_ref[to : to + WIDTH, :] = term[:, lanes(k)]

    def unmix(t):
        gain_sum = jnp.zeros((TILE, WIDTH), f32)
        for i in range(0, TILE, 2):
            at = slice((t * TILE + i) * TILE, (t * TILE + i + 2) * TILE)
            grad = work_ref[at, :WIDTH]
            centred = centred_ref[at, :]
            gain_sum += rows_sum(grad * centred)
            scaled = grad * gain
            mean = jnp.mean(scaled, axis=1, keepdims=True)
            mean_c = jnp.mean(scaled * centred, axis=1, keepdims=True)
            mixed = (scaled - mean - centred * mean_c) * inv_ref[at, :1]
            mixed_ref[t % 2, i : i + 2] = mixed.reshape(2, TILE, WIDTH)
        gain_sum_ref[...] += gain_sum
        for chunk in range(CHUNKS):
            grads = [mixed_ref[t % 2, i, :, lanes(chunk)] for i in range(TILE)]
            stem = []
            for i in range(0, TILE, 2):
                at = slice((t * TILE + i) * TILE, (t * TILE + i + 2) * TILE)
                pair = stem_ref[at, lanes(chunk)].astype(f32)
                stem += [pair[:TILE], pair[TILE:]]
            for col_tap in range(KERNEL):
                moved = column_shift(stem, col_tap - REACH)
                for row_tap in range(KERNEL):
                    total = None
                    for i in range(TILE):
                        source = i + row_tap - REACH
                        if 0 <= source < TILE:
                            part = moved[source] * grads[i]
                            total = part if total is None else total + part
                    taps_sum_ref[row_tap * KERNEL + col_tap, :, lanes(chunk)] += total
            inner = depthwise(grads, taps_ref, chunk, -1)
            for i in range(0, TILE, 2):
                at = slice((t * TILE + i) * TILE, (t * TILE + i + 2) * TILE)
                block = block_ref[at, lanes(chunk)]
                pair = jnp.concatenate([inner[i], inner[i + 1]], axis=0)
                gstem_ref[at, lanes(chunk)] = (block + pair).astype(bf16)

    parts = [(up_part, n) for n in range(0, INNER, 256)] + [(down_part, n) for n in range(0, INNER, 256)]
    for t in range(SLOTS):
        if t < len(parts):
            parts[t][0](parts[t][1])
        unmix(t)
    outs.append(copies.start(packed_ref.at[:STEM_AT], packed_hbm.at[:STEM_AT]))
    stem_term = over_positions(patches_ref[...], gstem_ref[...]).astype(bf16)
    scale_row = jnp.sum(scale_sum_ref[...], axis=0, keepdims=True) / layer
    small = jnp.concatenate(
        [
            jnp.sum(taps_sum_ref[...], axis=1),
            scale_row,
            jnp.sum(gain_sum_ref[...], axis=0, keepdims=True),
            jnp.zeros((SMALL_ROWS - KERNEL * KERNEL - 2, WIDTH), f32),
        ],
        axis=0,
    ).astype(bf16)
    for chunk in range(CHUNKS):
        to = STEM_AT + chunk * PATCH_CH
        packed_ref[to : to + PATCH_CH, :] = stem_term[:, lanes(chunk)]
        to = SMALL_AT + chunk * SMALL_ROWS
        packed_ref[to : to + SMALL_ROWS, :] = small[:, lanes(chunk)]
    packed_ref[PACK_USED:, :] = jnp.zeros((PACK_ROWS - PACK_USED, LANES), bf16)
    outs.append(copies.start(packed_ref.at[STEM_AT:], packed_hbm.at[STEM_AT:]))
    for out in outs:
        out.wait()


def backward(place, count, own, other, patches, stored, depth_w, gain, up, down, layer):
    vmem = pl.BlockSpec(memory_space=pltpu.VMEM)
    smem = pl.BlockSpec(memory_space=pltpu.SMEM)
    hbm = pl.BlockSpec(memory_space=pltpu.HBM)
    return pl.pallas_call(
        backward_kernel,
        out_shape=[
            pltpu.HBM((PACK_ROWS, LANES), bf16),
            jax.ShapeDtypeStruct((2 * N_DEC,), jnp.int32),
        ],
        in_specs=[smem, smem, vmem, vmem, vmem, hbm, hbm, hbm, hbm, hbm, vmem, hbm, hbm, vmem],
        out_specs=[hbm, smem],
        scratch_shapes=[
            pltpu.VMEM((POSITIONS, WIDTH), bf16),
            pltpu.VMEM((POSITIONS, WIDTH), f32),
            pltpu.VMEM((POSITIONS, LANES), f32),
            pltpu.VMEM((POSITIONS, INNER), f32),
            pltpu.VMEM((KERNEL * KERNEL, WIDTH), bf16),
            pltpu.VMEM((WIDTH, INNER), bf16),
            pltpu.VMEM((INNER, WIDTH), bf16),
            pltpu.VMEM((PACK_ROWS, LANES), bf16),
            pltpu.VMEM((KERNEL * KERNEL, WIDTH), f32),
            pltpu.VMEM((SEQ + 16, WIDTH), bf16),
            pltpu.VMEM((POSITIONS, WIDTH), f32),
            pltpu.VMEM((POSITIONS, WIDTH), bf16),
            pltpu.VMEM((POSITIONS, INNER), bf16),
            pltpu.VMEM((POSITIONS, INNER), f32),
            pltpu.VMEM((POSITIONS, INNER), bf16),
            pltpu.VMEM((POSITIONS, WIDTH), bf16),
            pltpu.VMEM((2, TILE, TILE, WIDTH), f32),
            pltpu.VMEM((POSITIONS, WIDTH), bf16),
            pltpu.VMEM((KERNEL * KERNEL, TILE, WIDTH), f32),
            pltpu.VMEM((TILE, WIDTH), f32),
            pltpu.VMEM((TILE, WIDTH), f32),
            pltpu.SemaphoreType.DMA((16,)),
        ],
        compiler_params=pltpu.CompilerParams(vmem_limit_bytes=VMEM_BYTES),
        cost_estimate=pl.CostEstimate(
            flops=8 * POSITIONS * WIDTH * INNER, bytes_accessed=10 << 20, transcendentals=0
        ),
        name="block_backward",
    )(
        place, count, own, other, patches, *map(in_hbm, stored), in_hbm(depth_w), gain,
        in_hbm(up), in_hbm(down), layer,
    )


def place_kernel(place_ref, spans_ref, feat_ref, out_ref, rows_ref):
    base = (2 * place_ref[0] + place_ref[1]) * SHARD
    rows_ref[...] = jnp.zeros((FEAT_TILE + SHARD + FEAT_TILE, WIDTH), f32)

    def one(k, carry):
        d = lax.div(k, SLOTS)
        j = k - d * SLOTS
        to = spans_ref[d] + FEAT_TILE * j - base

        @pl.when((j < spans_ref[N_DEC + d]) & (to > -FEAT_TILE) & (to < SHARD))
        def _():
            at = pl.ds(pl.multiple_of(j * FEAT_TILE, FEAT_TILE), FEAT_TILE)
            chunk = lax.div(to + FEAT_TILE, 16)
            row = lax.broadcasted_iota(jnp.int32, (32, FEAT_TILE), 0)
            col = lax.broadcasted_iota(jnp.int32, (32, FEAT_TILE), 1)
            pick = jnp.where(row == col + (to + FEAT_TILE - 16 * chunk), 1.0, 0.0).astype(bf16)
            window = pl.ds(pl.multiple_of(chunk * 16, 16), 32)
            rows_ref[window, :] += jnp.dot(pick, feat_ref[d, at, :], preferred_element_type=f32)

        return carry

    lax.fori_loop(0, N_DEC * SLOTS, one, 0)
    out_ref[...] = rows_ref[FEAT_TILE : FEAT_TILE + SHARD, :].astype(bf16)


def place_features(place, spans, feat):
    vmem = pl.BlockSpec(memory_space=pltpu.VMEM)
    smem = pl.BlockSpec(memory_space=pltpu.SMEM)
    return pl.pallas_call(
        place_kernel,
        out_shape=jax.ShapeDtypeStruct((SHARD, WIDTH), bf16),
        in_specs=[smem, smem, vmem],
        out_specs=vmem,
        scratch_shapes=[pltpu.VMEM((FEAT_TILE + SHARD + FEAT_TILE, WIDTH), f32)],
        compiler_params=pltpu.CompilerParams(vmem_limit_bytes=VMEM_BYTES),
        name="place_features",
    )(place, spans, feat)


def unpack_kernel(
    place_ref, own_ref, other_ref, stem_ref, depth_ref, gain_ref, up_ref, down_ref, scale_ref, rows_ref
):
    core = place_ref[1]
    factor = 1.0 / math.sqrt(N_OWNERS * MEAN_TILES * FEAT_TILE)
    rows_ref[pl.ds(pl.multiple_of(core * HALF_ROWS, 16), HALF_ROWS), :] = own_ref[...]
    rows_ref[pl.ds(pl.multiple_of((1 - core) * HALF_ROWS, 16), HALF_ROWS), :] = other_ref[...]

    def piece(at, count):
        return rows_ref[at : at + count, :].astype(f32) * factor

    for k in range(INNER // LANES):
        up_ref[:, lanes(k)] = piece(UP_AT + k * WIDTH, WIDTH)
    for chunk in range(CHUNKS):
        down_ref[:, lanes(chunk)] = piece(DOWN_AT + chunk * INNER, INNER)
        stem_ref[:, lanes(chunk)] = piece(STEM_AT + chunk * PATCH_CH, PATCH_CH)
        small = piece(SMALL_AT + chunk * SMALL_ROWS, SMALL_ROWS)
        taps = KERNEL * KERNEL
        depth_ref[:, lanes(chunk)] = small[:taps]
        scale_ref[lanes(chunk)] = small[taps]
        gain_ref[lanes(chunk)] = small[taps + 1]


def unpack(place, own, other):
    vmem = pl.BlockSpec(memory_space=pltpu.VMEM)
    smem = pl.BlockSpec(memory_space=pltpu.SMEM)
    shapes = (
        (PATCH_CH, WIDTH),
        (KERNEL * KERNEL, WIDTH),
        (WIDTH,),
        (WIDTH, INNER),
        (INNER, WIDTH),
        (WIDTH,),
    )
    return pl.pallas_call(
        unpack_kernel,
        out_shape=[jax.ShapeDtypeStruct(shape, f32) for shape in shapes],
        in_specs=[smem, vmem, vmem],
        out_specs=[vmem] * 6,
        scratch_shapes=[pltpu.VMEM((PACK_ROWS, LANES), bf16)],
        compiler_params=pltpu.CompilerParams(vmem_limit_bytes=VMEM_BYTES),
        name="unpack_terms",
    )(place, own, other)


def prepare_kernel(count_ref, gap_ref, embed_hbm, out_hbm, rows_ref, sems):
    copies = Copies(sems)
    rows_in = copies.start(embed_hbm.at[0], rows_ref.at[:SHARD])
    lane = lax.broadcasted_iota(jnp.int32, (16, WIDTH), 1)
    count, gap = count_ref[0, 0].astype(f32), gap_ref[0, 0].astype(f32)
    rows_ref[SHARD:, :] = jnp.where(lane == 0, count, jnp.where(lane == 1, gap, 0.0)).astype(bf16)
    rows_in.wait()
    outs = [copies.start(rows_ref, out_hbm.at[y]) for y in range(N_DEC // 2)]
    for out in outs:
        out.wait()


def prepare(tile_counts, text_gaps, embed_grad):
    smem = pl.BlockSpec(memory_space=pltpu.SMEM)
    hbm = pl.BlockSpec(memory_space=pltpu.HBM)
    return pl.pallas_call(
        prepare_kernel,
        out_shape=pltpu.HBM((N_DEC // 2, SHARD + 16, WIDTH), bf16),
        in_specs=[smem, smem, hbm],
        out_specs=hbm,
        scratch_shapes=[pltpu.VMEM((SHARD + 16, WIDTH), bf16), pltpu.SemaphoreType.DMA((8,))],
        compiler_params=pltpu.CompilerParams(vmem_limit_bytes=VMEM_BYTES),
        name="prepare_rows",
    )(tile_counts, text_gaps, in_hbm(embed_grad))


def swap_blocks(blocks, axes):
    return lax.all_to_all(blocks, axes, 0, 0, tiled=True)


def sum_blocks(blocks):
    return jnp.sum(blocks.astype(f32), axis=0).astype(bf16)


def spread(block, copies):
    return jnp.broadcast_to(block[None], (copies,) + block.shape)


def swap_cores(x):
    return lax.ppermute(x, "core", [(0, 1), (1, 0)])


def sum_all(packed, beside):
    half = sum_blocks(swap_blocks(packed.reshape(2, HALF_ROWS, LANES), "core"))
    part = sum_blocks(swap_blocks(half.reshape(16, PACK_ROWS // 32, LANES), PLANE))
    part = sum_blocks(swap_blocks(spread(part, 4), "zl"))
    part = sum_blocks(swap_blocks(spread(part, 4), "zh"))
    part, beside = lax.optimization_barrier((part, beside))
    return swap_blocks(spread(part, 16), PLANE).reshape(HALF_ROWS, LANES), beside


def on_device(
    pixels,
    tile_counts,
    text_gaps,
    stem_weight,
    depth_weight,
    norm_gain,
    up_weight,
    down_weight,
    layer_scale,
    embed_grad,
):
    place = jnp.stack([lax.axis_index("y"), lax.axis_index("core")]).astype(jnp.int32)
    count = tile_counts.reshape(1)
    gain = norm_gain.reshape(1, WIDTH)
    layer = layer_scale.reshape(1, WIDTH)
    patches = pixels.reshape(POSITIONS, PATCH_CH)
    own = swap_blocks(prepare(tile_counts, text_gaps, embed_grad), "y")
    *stored, feat = forward(
        count, patches, stem_weight, depth_weight, gain, up_weight, down_weight, layer
    )
    own, feat, place = lax.optimization_barrier((own, feat, place))
    other = swap_cores(own)
    feats = swap_blocks(feat, DEC)
    packed, spans = backward(
        place, count, own, other, patches, stored, depth_weight, gain, up_weight, down_weight, layer
    )
    packed, feats = lax.optimization_barrier((packed, feats))
    sequence = place_features(place, spans, feats)
    half, sequence = sum_all(packed, sequence)
    stem, depth, gain_grad, up, down, scale = unpack(place, half, swap_cores(half))
    return sequence[None], stem, depth, gain_grad, up, down, scale


def solution(mesh):
    fine = Mesh(mesh.devices.reshape(4, 4, 4, 4, 2), ("x", "zh", "zl", "y", "core"))
    return jax.shard_map(
        on_device,
        mesh=fine,
        in_specs=(
            P(DEC, ENC, None),
            P(DEC, ENC),
            P(DEC, ENC),
            P(),
            P(),
            P(),
            P(),
            P(),
            P(),
            P(ENC, DEC, None),
        ),
        out_specs=(P(ENC, DEC, None), P(), P(), P(), P(), P(), P()),
        check_vma=False,
    )
```

```python
import math

import jax
import jax.numpy as jnp
from jax import lax
from jax.experimental import pallas as pl
from jax.experimental.pallas import tpu as pltpu
from jax.sharding import Mesh
from jax.sharding import PartitionSpec as P

WIDTH = 384
INNER = 768
KERNEL = 7
REACH = KERNEL // 2
PATCH_CH = 48
TILE = 8
MEAN_TILES = 3
SLOTS = 9
FEAT_TILE = 16
N_OWNERS = 512
N_DEC = 8
SHARD = 208
SEQ = N_DEC * SHARD
POSITIONS = SLOTS * TILE * TILE
BLOCK_ROWS = SLOTS * FEAT_TILE
LANES = 128
LEAD = 8
LEAD_ROWS = LEAD * TILE * TILE
CHUNKS = WIDTH // LANES
PACK_ROWS = 5120
HALF_ROWS = PACK_ROWS // 2
UP_AT = 0
DOWN_AT = HALF_ROWS
LATE_AT = (INNER // LANES) * WIDTH
STEM_AT = LATE_AT
SMALL_AT = HALF_ROWS + LATE_AT
SMALL_ROWS = 64
DEC = ("y", "core")
ENC = ("x", "zh", "zl")
PLANE = ("x", "y")
VMEM_BYTES = 24 * 1024 * 1024

epsilon = 1e-06
GELU_A = math.sqrt(2.0 / math.pi)
GELU_B = 0.044715
bf16 = jnp.bfloat16
f32 = jnp.float32


def lanes(chunk):
    return slice(chunk * LANES, (chunk + 1) * LANES)


def column_shift(rows, step):
    if step == 0:
        return rows
    column = lax.broadcasted_iota(jnp.int32, (TILE, LANES), 0) + step
    inside = (column >= 0) & (column < TILE)
    return [jnp.where(inside, pltpu.roll(row, (-step) % TILE, 0), 0.0) for row in rows]


def depthwise(rows, taps_ref, chunk, sign):
    out = [jnp.zeros((TILE, LANES), f32)] * TILE
    for col_tap in range(KERNEL):
        moved = column_shift(rows, sign * (col_tap - REACH))
        for row_tap in range(KERNEL):
            weight = taps_ref[row_tap * KERNEL + col_tap, :, lanes(chunk)]
            for i in range(TILE):
                source = i + sign * (row_tap - REACH)
                if 0 <= source < TILE:
                    out[i] = out[i] + moved[source] * weight
    return out


def place_rows(i, j):
    return slice((i * TILE + j) * LEAD, (i * TILE + j + 1) * LEAD)


def last_rows(i):
    return slice(LEAD_ROWS + i * TILE, LEAD_ROWS + (i + 1) * TILE)


def depthwise_row(field_ref, taps_ref, chunk, sign, i):
    out = [jnp.zeros((LEAD, LANES), f32)] * TILE
    for row_tap in range(KERNEL):
        source = i + sign * (row_tap - REACH)
        if 0 <= source < TILE:
            row = [field_ref[place_rows(source, j), lanes(chunk)] for j in range(TILE)]
            for col_tap in range(KERNEL):
                weight = taps_ref[row_tap * KERNEL + col_tap, :, lanes(chunk)]
                for j in range(TILE):
                    column = j + sign * (col_tap - REACH)
                    if 0 <= column < TILE:
                        out[j] = out[j] + row[column] * weight
    return out


def set_taps(taps_ref, depth_w_ref):
    taps = depth_w_ref[...].astype(f32)
    for k in range(KERNEL * KERNEL):
        taps_ref[k] = jnp.broadcast_to(taps[k : k + 1], (TILE, WIDTH))


def in_hbm(x):
    return pltpu.with_memory_space_constraint(x, pltpu.HBM)


class Copies:
    def __init__(self, sems):
        self.sems, self.made = sems, []

    def start(self, source, target):
        copy = pltpu.make_async_copy(source, target, self.sems.at[len(self.made)])
        self.made.append(copy)
        copy.start()
        return copy


def forward_kernel(
    count_ref, patches_ref, stem_w_hbm, depth_w_hbm, gain_ref, up_hbm, down_hbm, layer_ref,
    stem_hbm, centred_hbm, hidden_hbm, inv_ref, feat_hbm,
    stem_w_ref, depth_w_ref, up_ref, down_ref, stem_ref, centred_ref, half_ref, hidden_ref,
    projected_ref, feat_ref, taps_ref, field_ref, mixed_ref, normed_ref, act_ref, pool_ref, last_ref,
    sems,
):
    copies = Copies(sems)
    stem_w_in = copies.start(stem_w_hbm, stem_w_ref)
    depth_w_in = copies.start(depth_w_hbm, depth_w_ref)
    up_in = copies.start(up_hbm, up_ref)
    down_in = copies.start(down_hbm, down_ref)
    outs = []
    stem_w_in.wait()
    stem = jnp.dot(patches_ref[...], stem_w_ref[...], preferred_element_type=f32).astype(bf16)
    stem_ref[...] = stem
    outs.append(copies.start(stem_ref, stem_hbm))
    field_ref[...] = stem.astype(f32)
    depth_w_in.wait()
    set_taps(taps_ref, depth_w_ref)
    gain = gain_ref[...]

    def norm(at):
        row = mixed_ref[at, :]
        deviation = row - jnp.mean(row, axis=1, keepdims=True)
        inv_std = lax.rsqrt(jnp.mean(deviation * deviation, axis=1, keepdims=True) + epsilon)
        centred = deviation * inv_std
        centred_ref[at, :] = centred
        inv_ref[at, :] = jnp.broadcast_to(inv_std, (2 * TILE, LANES))
        normed_ref[at, :] = (centred * gain).astype(bf16)

    for i in range(TILE):
        for chunk in range(CHUNKS):
            out = depthwise_row(field_ref, taps_ref, chunk, 1, i)
            for j in range(TILE):
                mixed_ref[place_rows(i, j), lanes(chunk)] = out[j]
        for at in range(i * 64, i * 64 + 64, 16):
            norm(slice(at, at + 16))
    for chunk in range(CHUNKS):
        out = depthwise([field_ref[last_rows(i), lanes(chunk)] for i in range(TILE)], taps_ref, chunk, 1)
        for i in range(TILE):
            mixed_ref[last_rows(i), lanes(chunk)] = out[i]
    for at in range(LEAD_ROWS, POSITIONS, 16):
        norm(slice(at, at + 16))
    outs.append(copies.start(centred_ref, centred_hbm))
    up_in.wait()
    normed = normed_ref[...]
    for n in range(0, INNER, 256):
        hidden_ref[:, n : n + 256] = jnp.dot(
            normed, up_ref[:, n : n + 256], preferred_element_type=f32
        )

    def activate(r, carry):
        at = pl.ds(pl.multiple_of(r * 16, 16), 16)
        v = hidden_ref[at, :]
        half_ref[at, :] = v.astype(bf16)
        t = jnp.tanh(GELU_A * (v + GELU_B * (v * v * v)))
        act_ref[at, :] = (0.5 * v * (1.0 + t)).astype(bf16)
        return carry

    lax.fori_loop(0, POSITIONS // 16, activate, 0, unroll=4)
    outs.append(copies.start(half_ref, hidden_hbm))
    down_in.wait()
    projected_ref[...] = jnp.dot(act_ref[...], down_ref[...], preferred_element_type=f32)
    layer = layer_ref[...]
    count = count_ref[0, 0]

    keep = jnp.where(lax.broadcasted_iota(jnp.int32, (LEAD, WIDTH), 0) < count, 0.25, 0.0)

    def block(at):
        return field_ref[at, :] + layer * projected_ref[at, :]

    for f in range(FEAT_TILE):
        i, j = 2 * (f // 4), 2 * (f % 4)
        total = block(place_rows(i, j)) + block(place_rows(i, j + 1))
        total += block(place_rows(i + 1, j)) + block(place_rows(i + 1, j + 1))
        pool_ref[f * LEAD : (f + 1) * LEAD, :] = total * keep
    keep_last = jnp.where(count == SLOTS, 0.25, 0.0).astype(f32)
    for pair in range(TILE // 2):
        total = block(last_rows(2 * pair)) + block(last_rows(2 * pair + 1))
        total = (total + pltpu.roll(total, TILE - 1, 0)) * keep_last
        for chunk in range(CHUNKS):
            last_ref[chunk, pair * TILE : (pair + 1) * TILE, :] = total[:, lanes(chunk)]
    for chunk in range(CHUNKS):
        pool_ref[LEAD * FEAT_TILE :, lanes(chunk)] = last_ref[chunk, pl.ds(0, FEAT_TILE, stride=2), :]
    row = lax.broadcasted_iota(jnp.int32, (BLOCK_ROWS, BLOCK_ROWS), 0)
    col = lax.broadcasted_iota(jnp.int32, (BLOCK_ROWS, BLOCK_ROWS), 1)
    tile, f = lax.shift_right_logical(row, 4), row & 15
    order = jnp.where(col == jnp.where(tile < LEAD, f * LEAD + tile, LEAD * FEAT_TILE + f), 1.0, 0.0)
    feat_ref[...] = jnp.dot(
        order.astype(bf16), pool_ref[...].astype(bf16), preferred_element_type=f32
    ).astype(bf16)
    for d in range(N_DEC):
        outs.append(copies.start(feat_ref, feat_hbm.at[d]))
    for out in outs:
        out.wait()


def forward(count, patches, stem_w, depth_w, gain, up, down, layer):
    vmem = pl.BlockSpec(memory_space=pltpu.VMEM)
    smem = pl.BlockSpec(memory_space=pltpu.SMEM)
    hbm = pl.BlockSpec(memory_space=pltpu.HBM)
    stored = (
        ((POSITIONS, WIDTH), bf16),
        ((POSITIONS, WIDTH), f32),
        ((POSITIONS, INNER), bf16),
    )
    inv = jax.ShapeDtypeStruct((POSITIONS, LANES), f32)
    return pl.pallas_call(
        forward_kernel,
        out_shape=[pltpu.HBM(*shape) for shape in stored] + [inv, pltpu.HBM((N_DEC, BLOCK_ROWS, WIDTH), bf16)],
        in_specs=[smem, vmem, hbm, hbm, vmem, hbm, hbm, vmem],
        out_specs=[hbm, hbm, hbm, vmem, hbm],
        scratch_shapes=[
            pltpu.VMEM((PATCH_CH, WIDTH), bf16),
            pltpu.VMEM((KERNEL * KERNEL, WIDTH), bf16),
            pltpu.VMEM((WIDTH, INNER), bf16),
            pltpu.VMEM((INNER, WIDTH), bf16),
            *[pltpu.VMEM(*shape) for shape in stored],
            pltpu.VMEM((POSITIONS, INNER), f32),
            pltpu.VMEM((POSITIONS, WIDTH), f32),
            pltpu.VMEM((BLOCK_ROWS, WIDTH), bf16),
            pltpu.VMEM((KERNEL * KERNEL, TILE, WIDTH), f32),
            pltpu.VMEM((POSITIONS, WIDTH), f32),
            pltpu.VMEM((POSITIONS, WIDTH), f32),
            pltpu.VMEM((POSITIONS, WIDTH), bf16),
            pltpu.VMEM((POSITIONS, INNER), bf16),
            pltpu.VMEM((BLOCK_ROWS, WIDTH), f32),
            pltpu.VMEM((CHUNKS, TILE // 2 * TILE, LANES), f32),
            pltpu.SemaphoreType.DMA((18,)),
        ],
        compiler_params=pltpu.CompilerParams(vmem_limit_bytes=VMEM_BYTES),
        cost_estimate=pl.CostEstimate(
            flops=4 * POSITIONS * WIDTH * INNER, bytes_accessed=8 << 20, transcendentals=0
        ),
        name="block_forward",
    )(count, patches, in_hbm(stem_w), in_hbm(depth_w), gain, in_hbm(up), in_hbm(down), layer)


def rows_times_rows(a, b):
    return lax.dot_general(a, b, (((1,), (1,)), ((), ())), preferred_element_type=f32)


def over_positions(a, b):
    return lax.dot_general(a, b, (((0,), (0,)), ((), ())), preferred_element_type=f32)


def rows_sum(x):
    return jnp.sum(x.reshape(-1, TILE, WIDTH), axis=0)


def backward_kernel(
    place_ref, own_ref, other_ref, patches_ref, stem_hbm, centred_hbm, hidden_hbm,
    inv_ref, depth_w_hbm, gain_ref, up_hbm, down_hbm, layer_ref,
    mine_hbm, theirs_hbm, spans_ref,
    stem_ref, centred_ref, hidden_ref, depth_w_ref, up_ref, down_ref, packed_ref,
    taps_ref, embed_ref, block_ref, proj_ref, act_ref, work_ref, ghid_ref, normed_ref, field_ref,
    mixed_ref, gstem_ref, taps_sum_ref, scale_sum_ref, tails_ref, sems,
):
    copies = Copies(sems)
    y_here, core_here = place_ref[0], place_ref[1]
    dec_here = 2 * y_here + core_here
    down_in = copies.start(down_hbm, down_ref)
    hidden_in = copies.start(hidden_hbm, hidden_ref)
    up_in = copies.start(up_hbm, up_ref)
    centred_in = copies.start(centred_hbm, centred_ref)
    depth_w_in = copies.start(depth_w_hbm, depth_w_ref)
    stem_in = copies.start(stem_hbm, stem_ref)
    outs = []
    layer = layer_ref[...]
    gain = gain_ref[...]
    scale_sum_ref[...] = jnp.zeros((TILE, WIDTH), f32)
    embed_ref[SEQ:, :] = jnp.zeros((16, WIDTH), bf16)
    for used in (STEM_AT + CHUNKS * PATCH_CH, SMALL_AT + CHUNKS * SMALL_ROWS):
        end = HALF_ROWS if used < HALF_ROWS else PACK_ROWS
        packed_ref[used:end, :] = jnp.zeros((end - used, LANES), bf16)
    counts, gaps = [None] * N_DEC, [None] * N_DEC
    for y in range(N_DEC // 2):
        for k, source in ((core_here, own_ref), (1 - core_here, other_ref)):
            to = pl.ds(pl.multiple_of((2 * y + k) * SHARD, 16), SHARD)
            embed_ref[to, :] = source[y, :SHARD, :]
            tails_ref[k, y] = source[y, SHARD:, :]
        for core in range(2):
            tail = tails_ref[core, y, :, :LANES].astype(f32)
            counts[2 * y + core] = tail[0, 0].astype(jnp.int32)
            gaps[2 * y + core] = tail[0, 1].astype(jnp.int32)
    at, own_offset, count = jnp.int32(0), jnp.int32(0), jnp.int32(0)
    for d in range(N_DEC):
        start = at + gaps[d]
        spans_ref[d] = start
        spans_ref[N_DEC + d] = counts[d]
        own_offset = jnp.where(dec_here == d, start, own_offset)
        count = jnp.where(dec_here == d, counts[d], count)
        at = start + FEAT_TILE * counts[d]

    base = lax.div(own_offset, 16)
    row = lax.broadcasted_iota(jnp.int32, (POSITIONS, BLOCK_ROWS + 16), 0)
    col = lax.broadcasted_iota(jnp.int32, (POSITIONS, BLOCK_ROWS + 16), 1)
    tile = jnp.where(row < LEAD_ROWS, row & (LEAD - 1), LEAD)
    spot = jnp.where(row < LEAD_ROWS, lax.shift_right_logical(row, 3), row - LEAD_ROWS)
    feat = lax.shift_right_logical(spot, 4) * 4 + (lax.shift_right_logical(spot, 1) & 3)
    hit = (col == tile * FEAT_TILE + feat + (own_offset - 16 * base)) & (tile < count)
    pick = jnp.where(hit, 0.25, 0.0).astype(bf16)
    window = embed_ref[pl.ds(pl.multiple_of(base * 16, 16), BLOCK_ROWS + 16), :]
    block = jnp.dot(pick, window, preferred_element_type=f32)
    block_ref[...] = block
    proj_ref[...] = (block * layer).astype(bf16)
    proj = proj_ref[...]
    down_in.wait()
    for n in range(0, INNER, 256):
        work_ref[:, n : n + 256] = rows_times_rows(proj, down_ref[n : n + 256, :])

    hidden_in.wait()

    def activate(r, carry):
        at = pl.ds(pl.multiple_of(r * 16, 16), 16)
        v = hidden_ref[at, :].astype(f32)
        square = v * v
        t = jnp.tanh(GELU_A * (v + GELU_B * (square * v)))
        half = 0.5 * (1.0 + t)
        act_ref[at, :] = (v * half).astype(bf16)
        slope = half + (0.5 * GELU_A) * v * (1.0 - t * t) * (1.0 + (3.0 * GELU_B) * square)
        ghid_ref[at, :] = (work_ref[at, :] * slope).astype(bf16)
        return carry

    lax.fori_loop(0, POSITIONS // 16, activate, 0, unroll=4)
    up_in.wait()
    work_ref[:, :WIDTH] = rows_times_rows(ghid_ref[...], up_ref[...])
    centred_in.wait()
    stem_in.wait()
    depth_w_in.wait()
    set_taps(taps_ref, depth_w_ref)
    field_ref[...] = stem_ref[...].astype(f32)

    def unnorm(r, carry):
        at = pl.ds(pl.multiple_of(r * 16, 16), 16)
        grad = work_ref[at, :WIDTH]
        centred = centred_ref[at, :]
        normed_ref[at, :] = (centred * gain).astype(bf16)
        scaled = grad * gain
        mean = jnp.mean(scaled, axis=1, keepdims=True)
        mean_c = jnp.mean(scaled * centred, axis=1, keepdims=True)
        mixed_ref[at, :] = (scaled - mean - centred * mean_c) * inv_ref[at, :1]
        return carry + rows_sum(grad * centred)

    gain_sum = lax.fori_loop(0, POSITIONS // 16, unnorm, jnp.zeros((TILE, WIDTH), f32), unroll=6)

    def down_part(n):
        term = over_positions(act_ref[:, n : n + 256], proj)
        scale_sum_ref[...] += rows_sum(term * down_ref[n : n + 256, :].astype(f32))
        term = term.astype(bf16)
        for chunk in range(CHUNKS):
            to = DOWN_AT + chunk * INNER + n
            packed_ref[to : to + 256, :] = term[:, lanes(chunk)]

    def up_part(n):
        term = over_positions(normed_ref[...], ghid_ref[:, n : n + 256]).astype(bf16)
        for k in range(2):
            to = UP_AT + (n // LANES + k) * WIDTH
            packed_ref[to : to + WIDTH, :] = term[:, lanes(k)]

    def taps_term(chunk, row_tap):
        sums = [jnp.zeros((LEAD, LANES), f32)] * KERNEL
        for i in range(TILE):
            source = i + row_tap - REACH
            if 0 <= source < TILE:
                row = [field_ref[place_rows(source, j), lanes(chunk)] for j in range(TILE)]
                for j in range(TILE):
                    grad = mixed_ref[place_rows(i, j), lanes(chunk)]
                    for col_tap in range(KERNEL):
                        column = j + col_tap - REACH
                        if 0 <= column < TILE:
                            sums[col_tap] = sums[col_tap] + row[column] * grad
        for col_tap in range(KERNEL):
            taps_sum_ref[row_tap * KERNEL + col_tap, :, lanes(chunk)] = sums[col_tap]

    def unmix_row(chunk, i):
        inner = depthwise_row(mixed_ref, taps_ref, chunk, -1, i)
        for j in range(0, TILE, 2):
            at = slice((i * TILE + j) * LEAD, (i * TILE + j + 2) * LEAD)
            pair = jnp.concatenate([inner[j], inner[j + 1]], axis=0)
            gstem_ref[at, lanes(chunk)] = (block_ref[at, lanes(chunk)] + pair).astype(bf16)

    def unmix_last(chunk):
        grads = [mixed_ref[last_rows(i), lanes(chunk)] for i in range(TILE)]
        stem = [field_ref[last_rows(i), lanes(chunk)] for i in range(TILE)]
        for col_tap in range(KERNEL):
            moved = column_shift(stem, col_tap - REACH)
            for row_tap in range(KERNEL):
                total = None
                for i in range(TILE):
                    source = i + row_tap - REACH
                    if 0 <= source < TILE:
                        part = moved[source] * grads[i]
                        total = part if total is None else total + part
                taps_sum_ref[row_tap * KERNEL + col_tap, :, lanes(chunk)] += total
        inner = depthwise(grads, taps_ref, chunk, -1)
        for i in range(0, TILE, 2):
            at = slice(LEAD_ROWS + i * TILE, LEAD_ROWS + (i + 2) * TILE)
            pair = jnp.concatenate([inner[i], inner[i + 1]], axis=0)
            gstem_ref[at, lanes(chunk)] = (block_ref[at, lanes(chunk)] + pair).astype(bf16)

    for n in range(0, INNER, 256):
        up_part(n)
        down_part(n)
    for core, target in ((core_here, mine_hbm), (1 - core_here, theirs_hbm)):
        at = pl.ds(pl.multiple_of(core * HALF_ROWS, 16), LATE_AT)
        outs.append(copies.start(packed_ref.at[at], target.at[:LATE_AT]))
    for chunk in range(CHUNKS):
        for row_tap in range(KERNEL):
            taps_term(chunk, row_tap)
        for i in range(TILE):
            unmix_row(chunk, i)
    for chunk in range(CHUNKS):
        unmix_last(chunk)
    stem_term = over_positions(patches_ref[...], gstem_ref[...]).astype(bf16)
    scale_row = jnp.sum(scale_sum_ref[...], axis=0, keepdims=True) / layer
    small = jnp.concatenate(
        [
            jnp.sum(taps_sum_ref[...], axis=1),
            scale_row,
            jnp.sum(gain_sum, axis=0, keepdims=True),
            jnp.zeros((SMALL_ROWS - KERNEL * KERNEL - 2, WIDTH), f32),
        ],
        axis=0,
    ).astype(bf16)
    for chunk in range(CHUNKS):
        to = STEM_AT + chunk * PATCH_CH
        packed_ref[to : to + PATCH_CH, :] = stem_term[:, lanes(chunk)]
        to = SMALL_AT + chunk * SMALL_ROWS
        packed_ref[to : to + SMALL_ROWS, :] = small[:, lanes(chunk)]
    for k, target in ((core_here, mine_hbm), (1 - core_here, theirs_hbm)):
        at = pl.ds(pl.multiple_of(k * HALF_ROWS + LATE_AT, 16), HALF_ROWS - LATE_AT)
        outs.append(copies.start(packed_ref.at[at], target.at[LATE_AT:]))
    for out in outs:
        out.wait()


def backward(place, own, other, patches, stored, depth_w, gain, up, down, layer):
    vmem = pl.BlockSpec(memory_space=pltpu.VMEM)
    smem = pl.BlockSpec(memory_space=pltpu.SMEM)
    hbm = pl.BlockSpec(memory_space=pltpu.HBM)
    return pl.pallas_call(
        backward_kernel,
        out_shape=[
            pltpu.HBM((HALF_ROWS, LANES), bf16),
            pltpu.HBM((HALF_ROWS, LANES), bf16),
            jax.ShapeDtypeStruct((2 * N_DEC,), jnp.int32),
        ],
        in_specs=[smem, vmem, vmem, vmem, hbm, hbm, hbm, vmem, hbm, vmem, hbm, hbm, vmem],
        out_specs=[hbm, hbm, smem],
        scratch_shapes=[
            pltpu.VMEM((POSITIONS, WIDTH), bf16),
            pltpu.VMEM((POSITIONS, WIDTH), f32),
            pltpu.VMEM((POSITIONS, INNER), bf16),
            pltpu.VMEM((KERNEL * KERNEL, WIDTH), bf16),
            pltpu.VMEM((WIDTH, INNER), bf16),
            pltpu.VMEM((INNER, WIDTH), bf16),
            pltpu.VMEM((PACK_ROWS, LANES), bf16),
            pltpu.VMEM((KERNEL * KERNEL, TILE, WIDTH), f32),
            pltpu.VMEM((SEQ + 16, WIDTH), bf16),
            pltpu.VMEM((POSITIONS, WIDTH), f32),
            pltpu.VMEM((POSITIONS, WIDTH), bf16),
            pltpu.VMEM((POSITIONS, INNER), bf16),
            pltpu.VMEM((POSITIONS, INNER), f32),
            pltpu.VMEM((POSITIONS, INNER), bf16),
            pltpu.VMEM((POSITIONS, WIDTH), bf16),
            pltpu.VMEM((POSITIONS, WIDTH), f32),
            pltpu.VMEM((POSITIONS, WIDTH), f32),
            pltpu.VMEM((POSITIONS, WIDTH), bf16),
            pltpu.VMEM((KERNEL * KERNEL, TILE, WIDTH), f32),
            pltpu.VMEM((TILE, WIDTH), f32),
            pltpu.VMEM((2, N_DEC // 2, 16, WIDTH), bf16),
            pltpu.SemaphoreType.DMA((24,)),
        ],
        compiler_params=pltpu.CompilerParams(vmem_limit_bytes=VMEM_BYTES),
        cost_estimate=pl.CostEstimate(
            flops=8 * POSITIONS * WIDTH * INNER, bytes_accessed=10 << 20, transcendentals=0
        ),
        name="block_backward",
    )(
        place, own, other, patches, *map(in_hbm, stored[:3]), stored[3], in_hbm(depth_w), gain,
        in_hbm(up), in_hbm(down), layer,
    )


def place_kernel(place_ref, spans_ref, feat_ref, out_ref, rows_ref):
    base = (2 * place_ref[0] + place_ref[1]) * SHARD
    rows_ref[...] = jnp.zeros((FEAT_TILE + SHARD + FEAT_TILE, WIDTH), f32)

    def one(k, carry):
        d = lax.div(k, SLOTS)
        j = k - d * SLOTS
        to = spans_ref[d] + FEAT_TILE * j - base

        @pl.when((j < spans_ref[N_DEC + d]) & (to > -FEAT_TILE) & (to < SHARD))
        def _():
            at = pl.ds(pl.multiple_of(j * FEAT_TILE, FEAT_TILE), FEAT_TILE)
            chunk = lax.div(to + FEAT_TILE, 16)
            row = lax.broadcasted_iota(jnp.int32, (32, FEAT_TILE), 0)
            col = lax.broadcasted_iota(jnp.int32, (32, FEAT_TILE), 1)
            pick = jnp.where(row == col + (to + FEAT_TILE - 16 * chunk), 1.0, 0.0).astype(bf16)
            window = pl.ds(pl.multiple_of(chunk * 16, 16), 32)
            rows_ref[window, :] += jnp.dot(pick, feat_ref[d, at, :], preferred_element_type=f32)

        return carry

    lax.fori_loop(0, N_DEC * SLOTS, one, 0)
    out_ref[...] = rows_ref[FEAT_TILE : FEAT_TILE + SHARD, :].astype(bf16)


def place_features(place, spans, feat):
    vmem = pl.BlockSpec(memory_space=pltpu.VMEM)
    smem = pl.BlockSpec(memory_space=pltpu.SMEM)
    return pl.pallas_call(
        place_kernel,
        out_shape=jax.ShapeDtypeStruct((SHARD, WIDTH), bf16),
        in_specs=[smem, smem, vmem],
        out_specs=vmem,
        scratch_shapes=[pltpu.VMEM((FEAT_TILE + SHARD + FEAT_TILE, WIDTH), f32)],
        compiler_params=pltpu.CompilerParams(vmem_limit_bytes=VMEM_BYTES),
        name="place_features",
    )(place, spans, feat)


def unpack_kernel(
    place_ref, own_ref, other_ref, stem_ref, depth_ref, gain_ref, up_ref, down_ref, scale_ref, rows_ref
):
    core = place_ref[1]
    factor = 1.0 / math.sqrt(N_OWNERS * MEAN_TILES * FEAT_TILE)
    rows_ref[pl.ds(pl.multiple_of(core * HALF_ROWS, 16), HALF_ROWS), :] = own_ref[...]
    rows_ref[pl.ds(pl.multiple_of((1 - core) * HALF_ROWS, 16), HALF_ROWS), :] = other_ref[...]

    def piece(at, count):
        return rows_ref[at : at + count, :].astype(f32) * factor

    for k in range(INNER // LANES):
        up_ref[:, lanes(k)] = piece(UP_AT + k * WIDTH, WIDTH)
    for chunk in range(CHUNKS):
        down_ref[:, lanes(chunk)] = piece(DOWN_AT + chunk * INNER, INNER)
        stem_ref[:, lanes(chunk)] = piece(STEM_AT + chunk * PATCH_CH, PATCH_CH)
        small = piece(SMALL_AT + chunk * SMALL_ROWS, SMALL_ROWS)
        taps = KERNEL * KERNEL
        depth_ref[:, lanes(chunk)] = small[:taps]
        scale_ref[lanes(chunk)] = small[taps]
        gain_ref[lanes(chunk)] = small[taps + 1]


def unpack(place, own, other):
    vmem = pl.BlockSpec(memory_space=pltpu.VMEM)
    smem = pl.BlockSpec(memory_space=pltpu.SMEM)
    shapes = (
        (PATCH_CH, WIDTH),
        (KERNEL * KERNEL, WIDTH),
        (WIDTH,),
        (WIDTH, INNER),
        (INNER, WIDTH),
        (WIDTH,),
    )
    return pl.pallas_call(
        unpack_kernel,
        out_shape=[jax.ShapeDtypeStruct(shape, f32) for shape in shapes],
        in_specs=[smem, vmem, vmem],
        out_specs=[vmem] * 6,
        scratch_shapes=[pltpu.VMEM((PACK_ROWS, LANES), bf16)],
        compiler_params=pltpu.CompilerParams(vmem_limit_bytes=VMEM_BYTES),
        name="unpack_terms",
    )(place, own, other)


def prepare_kernel(count_hbm, gap_hbm, embed_hbm, out_hbm, rows_ref, count_ref, gap_ref, sems):
    copies = Copies(sems)
    count_in = copies.start(count_hbm, count_ref)
    gap_in = copies.start(gap_hbm, gap_ref)
    rows_in = copies.start(embed_hbm.at[0], rows_ref.at[:SHARD])
    count_in.wait()
    gap_in.wait()
    lane = lax.broadcasted_iota(jnp.int32, (16, WIDTH), 1)
    count, gap = count_ref[0, 0].astype(f32), gap_ref[0, 0].astype(f32)
    rows_ref[SHARD:, :] = jnp.where(lane == 0, count, jnp.where(lane == 1, gap, 0.0)).astype(bf16)
    rows_in.wait()
    outs = [copies.start(rows_ref, out_hbm.at[y]) for y in range(N_DEC // 2)]
    for out in outs:
        out.wait()


def prepare(tile_counts, text_gaps, embed_grad):
    hbm = pl.BlockSpec(memory_space=pltpu.HBM)
    return pl.pallas_call(
        prepare_kernel,
        out_shape=pltpu.HBM((N_DEC // 2, SHARD + 16, WIDTH), bf16),
        in_specs=[pl.BlockSpec(memory_space=pl.ANY)] * 2 + [hbm],
        out_specs=hbm,
        scratch_shapes=[
            pltpu.VMEM((SHARD + 16, WIDTH), bf16),
            pltpu.SMEM((1, 1), jnp.int32),
            pltpu.SMEM((1, 1), jnp.int32),
            pltpu.SemaphoreType.DMA((8,)),
        ],
        compiler_params=pltpu.CompilerParams(vmem_limit_bytes=VMEM_BYTES),
        name="prepare_rows",
    )(tile_counts, text_gaps, in_hbm(embed_grad))


def swap_blocks(blocks, axes):
    return lax.all_to_all(blocks, axes, 0, 0, tiled=True)


def sum_blocks(blocks):
    return jnp.sum(blocks.astype(f32), axis=0).astype(bf16)


def spread(block, copies):
    return jnp.broadcast_to(block[None], (copies,) + block.shape)


def swap_cores(x):
    return lax.ppermute(x, "core", [(0, 1), (1, 0)])


def sum_all(half, beside):
    part = sum_blocks(swap_blocks(half.reshape(16, PACK_ROWS // 32, LANES), PLANE))
    part = sum_blocks(swap_blocks(spread(part, 4), "zl"))
    part = sum_blocks(swap_blocks(spread(part, 4), "zh"))
    part, beside = lax.optimization_barrier((part, beside))
    return swap_blocks(spread(part, 16), PLANE).reshape(HALF_ROWS, LANES), beside


def order_patches(tiles):
    patches = tiles.reshape(SLOTS, TILE * TILE, PATCH_CH)
    lead = patches[:LEAD].transpose(1, 0, 2).reshape(LEAD_ROWS, PATCH_CH)
    return jnp.concatenate([lead, patches[LEAD]])


def on_device(
    pixels,
    tile_counts,
    text_gaps,
    stem_weight,
    depth_weight,
    norm_gain,
    up_weight,
    down_weight,
    layer_scale,
    embed_grad,
):
    place = jnp.stack([lax.axis_index("y"), lax.axis_index("core")]).astype(jnp.int32)
    gain = norm_gain.reshape(1, WIDTH)
    layer = layer_scale.reshape(1, WIDTH)
    patches = order_patches(pixels[0])
    own = swap_blocks(prepare(tile_counts, text_gaps, embed_grad), "y")
    *stored, feat = forward(
        tile_counts, patches, stem_weight, depth_weight, gain, up_weight, down_weight, layer
    )
    own, feat, place = lax.optimization_barrier((own, feat, place))
    other = swap_cores(own)
    feats = swap_blocks(feat, DEC)
    mine, theirs, spans = backward(
        place, own, other, patches, stored, depth_weight, gain, up_weight, down_weight, layer
    )
    theirs, feats = lax.optimization_barrier((theirs, feats))
    half = (mine.astype(f32) + swap_cores(theirs).astype(f32)).astype(bf16)
    sequence = place_features(place, spans, feats)
    half, sequence = sum_all(half, sequence)
    stem, depth, gain_grad, up, down, scale = unpack(place, half, swap_cores(half))
    return sequence[None], stem, depth, gain_grad, up, down, scale


def solution(mesh):
    fine = Mesh(mesh.devices.reshape(4, 4, 4, 4, 2), ("x", "zh", "zl", "y", "core"))
    return jax.shard_map(
        on_device,
        mesh=fine,
        in_specs=(
            P(DEC, ENC, None),
            P(DEC, ENC),
            P(DEC, ENC),
            P(),
            P(),
            P(),
            P(),
            P(),
            P(),
            P(ENC, DEC, None),
        ),
        out_specs=(P(ENC, DEC, None), P(), P(), P(), P(), P(), P()),
        check_vma=False,
    )
```

```python
import math

import jax
import jax.numpy as jnp
from jax import lax
from jax.experimental import pallas as pl
from jax.experimental.pallas import tpu as pltpu
from jax.sharding import Mesh
from jax.sharding import PartitionSpec as P

WIDTH = 384
INNER = 768
KERNEL = 7
REACH = KERNEL // 2
PATCH_CH = 48
TILE = 8
MEAN_TILES = 3
SLOTS = 9
FEAT_TILE = 16
N_OWNERS = 512
N_DEC = 8
SHARD = 208
SEQ = N_DEC * SHARD
POSITIONS = SLOTS * TILE * TILE
BLOCK_ROWS = SLOTS * FEAT_TILE
LANES = 128
LEAD = 8
LEAD_ROWS = LEAD * TILE * TILE
CHUNKS = WIDTH // LANES
PACK_ROWS = 5120
HALF_ROWS = PACK_ROWS // 2
UP_AT = 0
DOWN_AT = HALF_ROWS
LATE_AT = (INNER // LANES) * WIDTH
STEM_AT = LATE_AT
SMALL_AT = HALF_ROWS + LATE_AT
SMALL_ROWS = 64
DEC = ("y", "core")
ENC = ("x", "z")
RUNS = [[4 * g + k for k in range(4)] for g in range(4)]
ACROSS = [[0, 6, 10, 12], [1, 7, 11, 13], [2, 4, 8, 14], [3, 5, 9, 15]]
PLANE = ("x", "y")
VMEM_BYTES = 24 * 1024 * 1024

epsilon = 1e-06
GELU_A = math.sqrt(2.0 / math.pi)
GELU_B = 0.044715
bf16 = jnp.bfloat16
f32 = jnp.float32


def lanes(chunk):
    return slice(chunk * LANES, (chunk + 1) * LANES)


def column_shift(rows, step):
    if step == 0:
        return rows
    column = lax.broadcasted_iota(jnp.int32, (TILE, LANES), 0) + step
    inside = (column >= 0) & (column < TILE)
    return [jnp.where(inside, pltpu.roll(row, (-step) % TILE, 0), 0.0) for row in rows]


def depthwise(rows, taps_ref, chunk, sign):
    out = [jnp.zeros((TILE, LANES), f32)] * TILE
    for col_tap in range(KERNEL):
        moved = column_shift(rows, sign * (col_tap - REACH))
        for row_tap in range(KERNEL):
            weight = taps_ref[row_tap * KERNEL + col_tap, :, lanes(chunk)]
            for i in range(TILE):
                source = i + sign * (row_tap - REACH)
                if 0 <= source < TILE:
                    out[i] = out[i] + moved[source] * weight
    return out


def place_rows(i, j):
    return slice((i * TILE + j) * LEAD, (i * TILE + j + 1) * LEAD)


def last_rows(i):
    return slice(LEAD_ROWS + i * TILE, LEAD_ROWS + (i + 1) * TILE)


def depthwise_row(field_ref, taps_ref, chunk, sign, i):
    out = [jnp.zeros((LEAD, LANES), f32)] * TILE
    for row_tap in range(KERNEL):
        source = i + sign * (row_tap - REACH)
        if 0 <= source < TILE:
            row = [field_ref[place_rows(source, j), lanes(chunk)] for j in range(TILE)]
            for col_tap in range(KERNEL):
                weight = taps_ref[row_tap * KERNEL + col_tap, :, lanes(chunk)]
                for j in range(TILE):
                    column = j + sign * (col_tap - REACH)
                    if 0 <= column < TILE:
                        out[j] = out[j] + row[column] * weight
    return out


def set_taps(taps_ref, depth_w_ref):
    taps = depth_w_ref[...].astype(f32)
    for k in range(KERNEL * KERNEL):
        taps_ref[k] = jnp.broadcast_to(taps[k : k + 1], (TILE, WIDTH))


def in_hbm(x):
    return pltpu.with_memory_space_constraint(x, pltpu.HBM)


class Copies:
    def __init__(self, sems):
        self.sems, self.made = sems, []

    def start(self, source, target):
        copy = pltpu.make_async_copy(source, target, self.sems.at[len(self.made)])
        self.made.append(copy)
        copy.start()
        return copy


def forward_kernel(
    count_ref, patches_ref, stem_w_hbm, depth_w_hbm, gain_ref, up_hbm, down_hbm, layer_ref,
    stem_hbm, centred_hbm, hidden_hbm, inv_ref, feat_hbm,
    stem_w_ref, depth_w_ref, up_ref, down_ref, stem_ref, centred_ref, half_ref, hidden_ref,
    projected_ref, feat_ref, taps_ref, field_ref, mixed_ref, normed_ref, act_ref, pool_ref, last_ref,
    sems,
):
    copies = Copies(sems)
    stem_w_in = copies.start(stem_w_hbm, stem_w_ref)
    depth_w_in = copies.start(depth_w_hbm, depth_w_ref)
    up_in = copies.start(up_hbm, up_ref)
    down_in = copies.start(down_hbm, down_ref)
    outs = []
    stem_w_in.wait()
    stem = jnp.dot(patches_ref[...], stem_w_ref[...], preferred_element_type=f32).astype(bf16)
    stem_ref[...] = stem
    outs.append(copies.start(stem_ref, stem_hbm))
    field_ref[...] = stem.astype(f32)
    depth_w_in.wait()
    set_taps(taps_ref, depth_w_ref)
    gain = gain_ref[...]

    def norm(at):
        row = mixed_ref[at, :]
        deviation = row - jnp.mean(row, axis=1, keepdims=True)
        inv_std = lax.rsqrt(jnp.mean(deviation * deviation, axis=1, keepdims=True) + epsilon)
        centred = deviation * inv_std
        centred_ref[at, :] = centred
        inv_ref[at, :] = jnp.broadcast_to(inv_std, (2 * TILE, LANES))
        normed_ref[at, :] = (centred * gain).astype(bf16)

    for i in range(TILE):
        for chunk in range(CHUNKS):
            out = depthwise_row(field_ref, taps_ref, chunk, 1, i)
            for j in range(TILE):
                mixed_ref[place_rows(i, j), lanes(chunk)] = out[j]
        for at in range(i * 64, i * 64 + 64, 16):
            norm(slice(at, at + 16))
    for chunk in range(CHUNKS):
        out = depthwise([field_ref[last_rows(i), lanes(chunk)] for i in range(TILE)], taps_ref, chunk, 1)
        for i in range(TILE):
            mixed_ref[last_rows(i), lanes(chunk)] = out[i]
    for at in range(LEAD_ROWS, POSITIONS, 16):
        norm(slice(at, at + 16))
    outs.append(copies.start(centred_ref, centred_hbm))
    up_in.wait()
    normed = normed_ref[...]
    for n in range(0, INNER, 256):
        hidden_ref[:, n : n + 256] = jnp.dot(
            normed, up_ref[:, n : n + 256], preferred_element_type=f32
        )

    def activate(r, carry):
        at = pl.ds(pl.multiple_of(r * 16, 16), 16)
        v = hidden_ref[at, :]
        half_ref[at, :] = v.astype(bf16)
        t = jnp.tanh(GELU_A * (v + GELU_B * (v * v * v)))
        act_ref[at, :] = (0.5 * v * (1.0 + t)).astype(bf16)
        return carry

    lax.fori_loop(0, POSITIONS // 16, activate, 0, unroll=4)
    outs.append(copies.start(half_ref, hidden_hbm))
    down_in.wait()
    projected_ref[...] = jnp.dot(act_ref[...], down_ref[...], preferred_element_type=f32)
    layer = layer_ref[...]
    count = count_ref[0, 0]

    keep = jnp.where(lax.broadcasted_iota(jnp.int32, (LEAD, WIDTH), 0) < count, 0.25, 0.0)

    def block(at):
        return field_ref[at, :] + layer * projected_ref[at, :]

    for f in range(FEAT_TILE):
        i, j = 2 * (f // 4), 2 * (f % 4)
        total = block(place_rows(i, j)) + block(place_rows(i, j + 1))
        total += block(place_rows(i + 1, j)) + block(place_rows(i + 1, j + 1))
        pool_ref[f * LEAD : (f + 1) * LEAD, :] = total * keep
    keep_last = jnp.where(count == SLOTS, 0.25, 0.0).astype(f32)
    for pair in range(TILE // 2):
        total = block(last_rows(2 * pair)) + block(last_rows(2 * pair + 1))
        total = (total + pltpu.roll(total, TILE - 1, 0)) * keep_last
        for chunk in range(CHUNKS):
            last_ref[chunk, pair * TILE : (pair + 1) * TILE, :] = total[:, lanes(chunk)]
    for chunk in range(CHUNKS):
        pool_ref[LEAD * FEAT_TILE :, lanes(chunk)] = last_ref[chunk, pl.ds(0, FEAT_TILE, stride=2), :]
    row = lax.broadcasted_iota(jnp.int32, (BLOCK_ROWS, BLOCK_ROWS), 0)
    col = lax.broadcasted_iota(jnp.int32, (BLOCK_ROWS, BLOCK_ROWS), 1)
    tile, f = lax.shift_right_logical(row, 4), row & 15
    order = jnp.where(col == jnp.where(tile < LEAD, f * LEAD + tile, LEAD * FEAT_TILE + f), 1.0, 0.0)
    feat_ref[...] = jnp.dot(
        order.astype(bf16), pool_ref[...].astype(bf16), preferred_element_type=f32
    ).astype(bf16)
    for d in range(N_DEC):
        outs.append(copies.start(feat_ref, feat_hbm.at[d]))
    for out in outs:
        out.wait()


def forward(count, patches, stem_w, depth_w, gain, up, down, layer):
    vmem = pl.BlockSpec(memory_space=pltpu.VMEM)
    smem = pl.BlockSpec(memory_space=pltpu.SMEM)
    hbm = pl.BlockSpec(memory_space=pltpu.HBM)
    stored = (
        ((POSITIONS, WIDTH), bf16),
        ((POSITIONS, WIDTH), f32),
        ((POSITIONS, INNER), bf16),
    )
    inv = jax.ShapeDtypeStruct((POSITIONS, LANES), f32)
    return pl.pallas_call(
        forward_kernel,
        out_shape=[pltpu.HBM(*shape) for shape in stored] + [inv, pltpu.HBM((N_DEC, BLOCK_ROWS, WIDTH), bf16)],
        in_specs=[smem, vmem, hbm, hbm, vmem, hbm, hbm, vmem],
        out_specs=[hbm, hbm, hbm, vmem, hbm],
        scratch_shapes=[
            pltpu.VMEM((PATCH_CH, WIDTH), bf16),
            pltpu.VMEM((KERNEL * KERNEL, WIDTH), bf16),
            pltpu.VMEM((WIDTH, INNER), bf16),
            pltpu.VMEM((INNER, WIDTH), bf16),
            *[pltpu.VMEM(*shape) for shape in stored],
            pltpu.VMEM((POSITIONS, INNER), f32),
            pltpu.VMEM((POSITIONS, WIDTH), f32),
            pltpu.VMEM((BLOCK_ROWS, WIDTH), bf16),
            pltpu.VMEM((KERNEL * KERNEL, TILE, WIDTH), f32),
            pltpu.VMEM((POSITIONS, WIDTH), f32),
            pltpu.VMEM((POSITIONS, WIDTH), f32),
            pltpu.VMEM((POSITIONS, WIDTH), bf16),
            pltpu.VMEM((POSITIONS, INNER), bf16),
            pltpu.VMEM((BLOCK_ROWS, WIDTH), f32),
            pltpu.VMEM((CHUNKS, TILE // 2 * TILE, LANES), f32),
            pltpu.SemaphoreType.DMA((18,)),
        ],
        compiler_params=pltpu.CompilerParams(vmem_limit_bytes=VMEM_BYTES),
        cost_estimate=pl.CostEstimate(
            flops=4 * POSITIONS * WIDTH * INNER, bytes_accessed=8 << 20, transcendentals=0
        ),
        name="block_forward",
    )(count, patches, in_hbm(stem_w), in_hbm(depth_w), gain, in_hbm(up), in_hbm(down), layer)


def rows_times_rows(a, b):
    return lax.dot_general(a, b, (((1,), (1,)), ((), ())), preferred_element_type=f32)


def over_positions(a, b):
    return lax.dot_general(a, b, (((0,), (0,)), ((), ())), preferred_element_type=f32)


def rows_sum(x):
    return jnp.sum(x.reshape(-1, TILE, WIDTH), axis=0)


def backward_kernel(
    place_ref, own_ref, other_ref, patches_ref, stem_hbm, centred_hbm, hidden_hbm,
    inv_ref, depth_w_hbm, gain_ref, up_hbm, down_hbm, layer_ref,
    mine_hbm, theirs_hbm, spans_ref,
    stem_ref, centred_ref, hidden_ref, depth_w_ref, up_ref, down_ref, packed_ref,
    taps_ref, embed_ref, block_ref, proj_ref, act_ref, work_ref, ghid_ref, normed_ref, field_ref,
    mixed_ref, gstem_ref, taps_sum_ref, scale_sum_ref, tails_ref, sems,
):
    copies = Copies(sems)
    y_here, core_here = place_ref[0], place_ref[1]
    dec_here = 2 * y_here + core_here
    down_in = copies.start(down_hbm, down_ref)
    hidden_in = copies.start(hidden_hbm, hidden_ref)
    up_in = copies.start(up_hbm, up_ref)
    centred_in = copies.start(centred_hbm, centred_ref)
    depth_w_in = copies.start(depth_w_hbm, depth_w_ref)
    stem_in = copies.start(stem_hbm, stem_ref)
    outs = []
    layer = layer_ref[...]
    gain = gain_ref[...]
    scale_sum_ref[...] = jnp.zeros((TILE, WIDTH), f32)
    embed_ref[SEQ:, :] = jnp.zeros((16, WIDTH), bf16)
    for used in (STEM_AT + CHUNKS * PATCH_CH, SMALL_AT + CHUNKS * SMALL_ROWS):
        end = HALF_ROWS if used < HALF_ROWS else PACK_ROWS
        packed_ref[used:end, :] = jnp.zeros((end - used, LANES), bf16)
    counts, gaps = [None] * N_DEC, [None] * N_DEC
    for y in range(N_DEC // 2):
        for k, source in ((core_here, own_ref), (1 - core_here, other_ref)):
            to = pl.ds(pl.multiple_of((2 * y + k) * SHARD, 16), SHARD)
            embed_ref[to, :] = source[y, :SHARD, :]
            tails_ref[k, y] = source[y, SHARD:, :]
        for core in range(2):
            tail = tails_ref[core, y, :, :LANES].astype(f32)
            counts[2 * y + core] = tail[0, 0].astype(jnp.int32)
            gaps[2 * y + core] = tail[0, 1].astype(jnp.int32)
    at, own_offset, count = jnp.int32(0), jnp.int32(0), jnp.int32(0)
    for d in range(N_DEC):
        start = at + gaps[d]
        spans_ref[d] = start
        spans_ref[N_DEC + d] = counts[d]
        own_offset = jnp.where(dec_here == d, start, own_offset)
        count = jnp.where(dec_here == d, counts[d], count)
        at = start + FEAT_TILE * counts[d]

    base = lax.div(own_offset, 16)
    row = lax.broadcasted_iota(jnp.int32, (POSITIONS, BLOCK_ROWS + 16), 0)
    col = lax.broadcasted_iota(jnp.int32, (POSITIONS, BLOCK_ROWS + 16), 1)
    tile = jnp.where(row < LEAD_ROWS, row & (LEAD - 1), LEAD)
    spot = jnp.where(row < LEAD_ROWS, lax.shift_right_logical(row, 3), row - LEAD_ROWS)
    feat = lax.shift_right_logical(spot, 4) * 4 + (lax.shift_right_logical(spot, 1) & 3)
    hit = (col == tile * FEAT_TILE + feat + (own_offset - 16 * base)) & (tile < count)
    pick = jnp.where(hit, 0.25, 0.0).astype(bf16)
    window = embed_ref[pl.ds(pl.multiple_of(base * 16, 16), BLOCK_ROWS + 16), :]
    block = jnp.dot(pick, window, preferred_element_type=f32)
    block_ref[...] = block
    proj_ref[...] = (block * layer).astype(bf16)
    proj = proj_ref[...]
    down_in.wait()
    for n in range(0, INNER, 256):
        work_ref[:, n : n + 256] = rows_times_rows(proj, down_ref[n : n + 256, :])

    hidden_in.wait()

    def activate(r, carry):
        at = pl.ds(pl.multiple_of(r * 16, 16), 16)
        v = hidden_ref[at, :].astype(f32)
        square = v * v
        t = jnp.tanh(GELU_A * (v + GELU_B * (square * v)))
        half = 0.5 * (1.0 + t)
        act_ref[at, :] = (v * half).astype(bf16)
        slope = half + (0.5 * GELU_A) * v * (1.0 - t * t) * (1.0 + (3.0 * GELU_B) * square)
        ghid_ref[at, :] = (work_ref[at, :] * slope).astype(bf16)
        return carry

    lax.fori_loop(0, POSITIONS // 16, activate, 0, unroll=4)
    up_in.wait()
    work_ref[:, :WIDTH] = rows_times_rows(ghid_ref[...], up_ref[...])
    centred_in.wait()
    stem_in.wait()
    depth_w_in.wait()
    set_taps(taps_ref, depth_w_ref)
    field_ref[...] = stem_ref[...].astype(f32)

    def unnorm(r, carry):
        at = pl.ds(pl.multiple_of(r * 16, 16), 16)
        grad = work_ref[at, :WIDTH]
        centred = centred_ref[at, :]
        normed_ref[at, :] = (centred * gain).astype(bf16)
        scaled = grad * gain
        mean = jnp.mean(scaled, axis=1, keepdims=True)
        mean_c = jnp.mean(scaled * centred, axis=1, keepdims=True)
        mixed_ref[at, :] = (scaled - mean - centred * mean_c) * inv_ref[at, :1]
        return carry + rows_sum(grad * centred)

    gain_sum = lax.fori_loop(0, POSITIONS // 16, unnorm, jnp.zeros((TILE, WIDTH), f32), unroll=6)

    def down_part(n):
        term = over_positions(act_ref[:, n : n + 256], proj)
        scale_sum_ref[...] += rows_sum(term * down_ref[n : n + 256, :].astype(f32))
        term = term.astype(bf16)
        for chunk in range(CHUNKS):
            to = DOWN_AT + chunk * INNER + n
            packed_ref[to : to + 256, :] = term[:, lanes(chunk)]

    def up_part(n):
        term = over_positions(normed_ref[...], ghid_ref[:, n : n + 256]).astype(bf16)
        for k in range(2):
            to = UP_AT + (n // LANES + k) * WIDTH
            packed_ref[to : to + WIDTH, :] = term[:, lanes(k)]

    def taps_term(chunk, row_tap):
        sums = [jnp.zeros((LEAD, LANES), f32)] * KERNEL
        for i in range(TILE):
            source = i + row_tap - REACH
            if 0 <= source < TILE:
                row = [field_ref[place_rows(source, j), lanes(chunk)] for j in range(TILE)]
                for j in range(TILE):
                    grad = mixed_ref[place_rows(i, j), lanes(chunk)]
                    for col_tap in range(KERNEL):
                        column = j + col_tap - REACH
                        if 0 <= column < TILE:
                            sums[col_tap] = sums[col_tap] + row[column] * grad
        for col_tap in range(KERNEL):
            taps_sum_ref[row_tap * KERNEL + col_tap, :, lanes(chunk)] = sums[col_tap]

    def unmix_row(chunk, i):
        inner = depthwise_row(mixed_ref, taps_ref, chunk, -1, i)
        for j in range(0, TILE, 2):
            at = slice((i * TILE + j) * LEAD, (i * TILE + j + 2) * LEAD)
            pair = jnp.concatenate([inner[j], inner[j + 1]], axis=0)
            gstem_ref[at, lanes(chunk)] = (block_ref[at, lanes(chunk)] + pair).astype(bf16)

    def unmix_last(chunk):
        grads = [mixed_ref[last_rows(i), lanes(chunk)] for i in range(TILE)]
        stem = [field_ref[last_rows(i), lanes(chunk)] for i in range(TILE)]
        for col_tap in range(KERNEL):
            moved = column_shift(stem, col_tap - REACH)
            for row_tap in range(KERNEL):
                total = None
                for i in range(TILE):
                    source = i + row_tap - REACH
                    if 0 <= source < TILE:
                        part = moved[source] * grads[i]
                        total = part if total is None else total + part
                taps_sum_ref[row_tap * KERNEL + col_tap, :, lanes(chunk)] += total
        inner = depthwise(grads, taps_ref, chunk, -1)
        for i in range(0, TILE, 2):
            at = slice(LEAD_ROWS + i * TILE, LEAD_ROWS + (i + 2) * TILE)
            pair = jnp.concatenate([inner[i], inner[i + 1]], axis=0)
            gstem_ref[at, lanes(chunk)] = (block_ref[at, lanes(chunk)] + pair).astype(bf16)

    for n in range(0, INNER, 256):
        up_part(n)
        down_part(n)
    for core, target in ((core_here, mine_hbm), (1 - core_here, theirs_hbm)):
        at = pl.ds(pl.multiple_of(core * HALF_ROWS, 16), LATE_AT)
        outs.append(copies.start(packed_ref.at[at], target.at[:LATE_AT]))
    for chunk in range(CHUNKS):
        for row_tap in range(KERNEL):
            taps_term(chunk, row_tap)
        for i in range(TILE):
            unmix_row(chunk, i)
    for chunk in range(CHUNKS):
        unmix_last(chunk)
    stem_term = over_positions(patches_ref[...], gstem_ref[...]).astype(bf16)
    scale_row = jnp.sum(scale_sum_ref[...], axis=0, keepdims=True) / layer
    small = jnp.concatenate(
        [
            jnp.sum(taps_sum_ref[...], axis=1),
            scale_row,
            jnp.sum(gain_sum, axis=0, keepdims=True),
            jnp.zeros((SMALL_ROWS - KERNEL * KERNEL - 2, WIDTH), f32),
        ],
        axis=0,
    ).astype(bf16)
    for chunk in range(CHUNKS):
        to = STEM_AT + chunk * PATCH_CH
        packed_ref[to : to + PATCH_CH, :] = stem_term[:, lanes(chunk)]
        to = SMALL_AT + chunk * SMALL_ROWS
        packed_ref[to : to + SMALL_ROWS, :] = small[:, lanes(chunk)]
    for k, target in ((core_here, mine_hbm), (1 - core_here, theirs_hbm)):
        at = pl.ds(pl.multiple_of(k * HALF_ROWS + LATE_AT, 16), HALF_ROWS - LATE_AT)
        outs.append(copies.start(packed_ref.at[at], target.at[LATE_AT:]))
    for out in outs:
        out.wait()


def backward(place, own, other, patches, stored, depth_w, gain, up, down, layer):
    vmem = pl.BlockSpec(memory_space=pltpu.VMEM)
    smem = pl.BlockSpec(memory_space=pltpu.SMEM)
    hbm = pl.BlockSpec(memory_space=pltpu.HBM)
    return pl.pallas_call(
        backward_kernel,
        out_shape=[
            pltpu.HBM((HALF_ROWS, LANES), bf16),
            pltpu.HBM((HALF_ROWS, LANES), bf16),
            jax.ShapeDtypeStruct((2 * N_DEC,), jnp.int32),
        ],
        in_specs=[smem, vmem, vmem, vmem, hbm, hbm, hbm, vmem, hbm, vmem, hbm, hbm, vmem],
        out_specs=[hbm, hbm, smem],
        scratch_shapes=[
            pltpu.VMEM((POSITIONS, WIDTH), bf16),
            pltpu.VMEM((POSITIONS, WIDTH), f32),
            pltpu.VMEM((POSITIONS, INNER), bf16),
            pltpu.VMEM((KERNEL * KERNEL, WIDTH), bf16),
            pltpu.VMEM((WIDTH, INNER), bf16),
            pltpu.VMEM((INNER, WIDTH), bf16),
            pltpu.VMEM((PACK_ROWS, LANES), bf16),
            pltpu.VMEM((KERNEL * KERNEL, TILE, WIDTH), f32),
            pltpu.VMEM((SEQ + 16, WIDTH), bf16),
            pltpu.VMEM((POSITIONS, WIDTH), f32),
            pltpu.VMEM((POSITIONS, WIDTH), bf16),
            pltpu.VMEM((POSITIONS, INNER), bf16),
            pltpu.VMEM((POSITIONS, INNER), f32),
            pltpu.VMEM((POSITIONS, INNER), bf16),
            pltpu.VMEM((POSITIONS, WIDTH), bf16),
            pltpu.VMEM((POSITIONS, WIDTH), f32),
            pltpu.VMEM((POSITIONS, WIDTH), f32),
            pltpu.VMEM((POSITIONS, WIDTH), bf16),
            pltpu.VMEM((KERNEL * KERNEL, TILE, WIDTH), f32),
            pltpu.VMEM((TILE, WIDTH), f32),
            pltpu.VMEM((2, N_DEC // 2, 16, WIDTH), bf16),
            pltpu.SemaphoreType.DMA((24,)),
        ],
        compiler_params=pltpu.CompilerParams(vmem_limit_bytes=VMEM_BYTES),
        cost_estimate=pl.CostEstimate(
            flops=8 * POSITIONS * WIDTH * INNER, bytes_accessed=10 << 20, transcendentals=0
        ),
        name="block_backward",
    )(
        place, own, other, patches, *map(in_hbm, stored[:3]), stored[3], in_hbm(depth_w), gain,
        in_hbm(up), in_hbm(down), layer,
    )


def place_kernel(place_ref, spans_ref, feat_ref, out_ref, rows_ref):
    base = (2 * place_ref[0] + place_ref[1]) * SHARD
    rows_ref[...] = jnp.zeros((FEAT_TILE + SHARD + FEAT_TILE, WIDTH), f32)

    def one(k, carry):
        d = lax.div(k, SLOTS)
        j = k - d * SLOTS
        to = spans_ref[d] + FEAT_TILE * j - base

        @pl.when((j < spans_ref[N_DEC + d]) & (to > -FEAT_TILE) & (to < SHARD))
        def _():
            at = pl.ds(pl.multiple_of(j * FEAT_TILE, FEAT_TILE), FEAT_TILE)
            chunk = lax.div(to + FEAT_TILE, 16)
            row = lax.broadcasted_iota(jnp.int32, (32, FEAT_TILE), 0)
            col = lax.broadcasted_iota(jnp.int32, (32, FEAT_TILE), 1)
            pick = jnp.where(row == col + (to + FEAT_TILE - 16 * chunk), 1.0, 0.0).astype(bf16)
            window = pl.ds(pl.multiple_of(chunk * 16, 16), 32)
            rows_ref[window, :] += jnp.dot(pick, feat_ref[d, at, :], preferred_element_type=f32)

        return carry

    lax.fori_loop(0, N_DEC * SLOTS, one, 0)
    out_ref[...] = rows_ref[FEAT_TILE : FEAT_TILE + SHARD, :].astype(bf16)


def place_features(place, spans, feat):
    vmem = pl.BlockSpec(memory_space=pltpu.VMEM)
    smem = pl.BlockSpec(memory_space=pltpu.SMEM)
    return pl.pallas_call(
        place_kernel,
        out_shape=jax.ShapeDtypeStruct((SHARD, WIDTH), bf16),
        in_specs=[smem, smem, vmem],
        out_specs=vmem,
        scratch_shapes=[pltpu.VMEM((FEAT_TILE + SHARD + FEAT_TILE, WIDTH), f32)],
        compiler_params=pltpu.CompilerParams(vmem_limit_bytes=VMEM_BYTES),
        name="place_features",
    )(place, spans, feat)


def unpack_kernel(
    place_ref, own_ref, other_ref, stem_ref, depth_ref, gain_ref, up_ref, down_ref, scale_ref, rows_ref
):
    core = place_ref[1]
    factor = 1.0 / math.sqrt(N_OWNERS * MEAN_TILES * FEAT_TILE)
    rows_ref[pl.ds(pl.multiple_of(core * HALF_ROWS, 16), HALF_ROWS), :] = own_ref[...]
    rows_ref[pl.ds(pl.multiple_of((1 - core) * HALF_ROWS, 16), HALF_ROWS), :] = other_ref[...]

    def piece(at, count):
        return rows_ref[at : at + count, :].astype(f32) * factor

    for k in range(INNER // LANES):
        up_ref[:, lanes(k)] = piece(UP_AT + k * WIDTH, WIDTH)
    for chunk in range(CHUNKS):
        down_ref[:, lanes(chunk)] = piece(DOWN_AT + chunk * INNER, INNER)
        stem_ref[:, lanes(chunk)] = piece(STEM_AT + chunk * PATCH_CH, PATCH_CH)
        small = piece(SMALL_AT + chunk * SMALL_ROWS, SMALL_ROWS)
        taps = KERNEL * KERNEL
        depth_ref[:, lanes(chunk)] = small[:taps]
        scale_ref[lanes(chunk)] = small[taps]
        gain_ref[lanes(chunk)] = small[taps + 1]


def unpack(place, own, other):
    vmem = pl.BlockSpec(memory_space=pltpu.VMEM)
    smem = pl.BlockSpec(memory_space=pltpu.SMEM)
    shapes = (
        (PATCH_CH, WIDTH),
        (KERNEL * KERNEL, WIDTH),
        (WIDTH,),
        (WIDTH, INNER),
        (INNER, WIDTH),
        (WIDTH,),
    )
    return pl.pallas_call(
        unpack_kernel,
        out_shape=[jax.ShapeDtypeStruct(shape, f32) for shape in shapes],
        in_specs=[smem, vmem, vmem],
        out_specs=[vmem] * 6,
        scratch_shapes=[pltpu.VMEM((PACK_ROWS, LANES), bf16)],
        compiler_params=pltpu.CompilerParams(vmem_limit_bytes=VMEM_BYTES),
        name="unpack_terms",
    )(place, own, other)


def prepare_kernel(count_hbm, gap_hbm, embed_hbm, out_hbm, rows_ref, count_ref, gap_ref, sems):
    copies = Copies(sems)
    count_in = copies.start(count_hbm, count_ref)
    gap_in = copies.start(gap_hbm, gap_ref)
    rows_in = copies.start(embed_hbm.at[0], rows_ref.at[:SHARD])
    count_in.wait()
    gap_in.wait()
    lane = lax.broadcasted_iota(jnp.int32, (16, WIDTH), 1)
    count, gap = count_ref[0, 0].astype(f32), gap_ref[0, 0].astype(f32)
    rows_ref[SHARD:, :] = jnp.where(lane == 0, count, jnp.where(lane == 1, gap, 0.0)).astype(bf16)
    rows_in.wait()
    outs = [copies.start(rows_ref, out_hbm.at[y]) for y in range(N_DEC // 2)]
    for out in outs:
        out.wait()


def prepare(tile_counts, text_gaps, embed_grad):
    hbm = pl.BlockSpec(memory_space=pltpu.HBM)
    return pl.pallas_call(
        prepare_kernel,
        out_shape=pltpu.HBM((N_DEC // 2, SHARD + 16, WIDTH), bf16),
        in_specs=[pl.BlockSpec(memory_space=pl.ANY)] * 2 + [hbm],
        out_specs=hbm,
        scratch_shapes=[
            pltpu.VMEM((SHARD + 16, WIDTH), bf16),
            pltpu.SMEM((1, 1), jnp.int32),
            pltpu.SMEM((1, 1), jnp.int32),
            pltpu.SemaphoreType.DMA((8,)),
        ],
        compiler_params=pltpu.CompilerParams(vmem_limit_bytes=VMEM_BYTES),
        name="prepare_rows",
    )(tile_counts, text_gaps, in_hbm(embed_grad))


def swap_blocks(blocks, axes, groups=None):
    return lax.all_to_all(blocks, axes, 0, 0, axis_index_groups=groups, tiled=True)


def sum_blocks(blocks):
    return jnp.sum(blocks.astype(f32), axis=0).astype(bf16)


def spread(block, copies):
    return jnp.broadcast_to(block[None], (copies,) + block.shape)


def swap_cores(x):
    return lax.ppermute(x, "core", [(0, 1), (1, 0)])


def sum_all(half, beside):
    part = sum_blocks(swap_blocks(half.reshape(16, PACK_ROWS // 32, LANES), PLANE))
    part = sum_blocks(swap_blocks(spread(part, 4), "z", RUNS))
    part = sum_blocks(swap_blocks(spread(part, 4), "z", ACROSS))
    part, beside = lax.optimization_barrier((part, beside))
    return swap_blocks(spread(part, 16), PLANE).reshape(HALF_ROWS, LANES), beside


def order_patches(tiles):
    patches = tiles.reshape(SLOTS, TILE * TILE, PATCH_CH)
    lead = patches[:LEAD].transpose(1, 0, 2).reshape(LEAD_ROWS, PATCH_CH)
    return jnp.concatenate([lead, patches[LEAD]])


def on_device(
    pixels,
    tile_counts,
    text_gaps,
    stem_weight,
    depth_weight,
    norm_gain,
    up_weight,
    down_weight,
    layer_scale,
    embed_grad,
):
    place = jnp.stack([lax.axis_index("y"), lax.axis_index("core")]).astype(jnp.int32)
    gain = norm_gain.reshape(1, WIDTH)
    layer = layer_scale.reshape(1, WIDTH)
    patches = order_patches(pixels[0])
    own = swap_blocks(prepare(tile_counts, text_gaps, embed_grad), "y")
    *stored, feat = forward(
        tile_counts, patches, stem_weight, depth_weight, gain, up_weight, down_weight, layer
    )
    own, feat, place = lax.optimization_barrier((own, feat, place))
    other = swap_cores(own)
    feats = swap_blocks(feat, DEC)
    mine, theirs, spans = backward(
        place, own, other, patches, stored, depth_weight, gain, up_weight, down_weight, layer
    )
    theirs, feats = lax.optimization_barrier((theirs, feats))
    half = (mine.astype(f32) + swap_cores(theirs).astype(f32)).astype(bf16)
    sequence = place_features(place, spans, feats)
    half, sequence = sum_all(half, sequence)
    stem, depth, gain_grad, up, down, scale = unpack(place, half, swap_cores(half))
    return sequence[None], stem, depth, gain_grad, up, down, scale


def solution(mesh):
    fine = Mesh(mesh.devices.reshape(4, 16, 4, 2), ("x", "z", "y", "core"))
    return jax.shard_map(
        on_device,
        mesh=fine,
        in_specs=(
            P(DEC, ENC, None),
            P(DEC, ENC),
            P(DEC, ENC),
            P(),
            P(),
            P(),
            P(),
            P(),
            P(),
            P(ENC, DEC, None),
        ),
        out_specs=(P(ENC, DEC, None), P(), P(), P(), P(), P(), P()),
        check_vma=False,
    )
```

```python
import math

import jax
import jax.numpy as jnp
from jax import lax
from jax.experimental import pallas as pl
from jax.experimental.pallas import tpu as pltpu
from jax.sharding import Mesh
from jax.sharding import PartitionSpec as P

WIDTH = 384
INNER = 768
KERNEL = 7
REACH = KERNEL // 2
PATCH_CH = 48
TILE = 8
MEAN_TILES = 3
SLOTS = 9
FEAT_TILE = 16
N_OWNERS = 512
N_DEC = 8
SHARD = 208
SEQ = N_DEC * SHARD
POSITIONS = SLOTS * TILE * TILE
BLOCK_ROWS = SLOTS * FEAT_TILE
LANES = 128
LEAD = 8
LEAD_ROWS = LEAD * TILE * TILE
CHUNKS = WIDTH // LANES
PACK_ROWS = 5120
HALF_ROWS = PACK_ROWS // 2
UP_AT = 0
DOWN_AT = HALF_ROWS
LATE_AT = (INNER // LANES) * WIDTH
STEM_AT = LATE_AT
SMALL_AT = HALF_ROWS + LATE_AT
SMALL_ROWS = 64
DEC = ("y", "core")
ENC = ("x", "pair", "side")
BLOCK = ("x", "pair", "side", "y")
BLOCKS = [
    [((x * 8 + pair) * 2 + (side if pair < 4 else 1 - side)) * 4 + y for x in range(4) for y in range(4) for side in range(2)]
    for pair in range(8)
]
ACROSS = [[0, 2, 4, 6, 9, 11, 13, 15], [1, 3, 5, 7, 8, 10, 12, 14]]
VMEM_BYTES = 24 * 1024 * 1024

epsilon = 1e-06
GELU_A = math.sqrt(2.0 / math.pi)
GELU_B = 0.044715
bf16 = jnp.bfloat16
f32 = jnp.float32


def lanes(chunk):
    return slice(chunk * LANES, (chunk + 1) * LANES)


def column_shift(rows, step):
    if step == 0:
        return rows
    column = lax.broadcasted_iota(jnp.int32, (TILE, LANES), 0) + step
    inside = (column >= 0) & (column < TILE)
    return [jnp.where(inside, pltpu.roll(row, (-step) % TILE, 0), 0.0) for row in rows]


def depthwise(rows, taps_ref, chunk, sign):
    out = [jnp.zeros((TILE, LANES), f32)] * TILE
    for col_tap in range(KERNEL):
        moved = column_shift(rows, sign * (col_tap - REACH))
        for row_tap in range(KERNEL):
            weight = taps_ref[row_tap * KERNEL + col_tap, :, lanes(chunk)]
            for i in range(TILE):
                source = i + sign * (row_tap - REACH)
                if 0 <= source < TILE:
                    out[i] = out[i] + moved[source] * weight
    return out


def place_rows(i, j):
    return slice((i * TILE + j) * LEAD, (i * TILE + j + 1) * LEAD)


def last_rows(i):
    return slice(LEAD_ROWS + i * TILE, LEAD_ROWS + (i + 1) * TILE)


def depthwise_row(field_ref, taps_ref, chunk, sign, i):
    out = [jnp.zeros((LEAD, LANES), f32)] * TILE
    for row_tap in range(KERNEL):
        source = i + sign * (row_tap - REACH)
        if 0 <= source < TILE:
            row = [field_ref[place_rows(source, j), lanes(chunk)] for j in range(TILE)]
            for col_tap in range(KERNEL):
                weight = taps_ref[row_tap * KERNEL + col_tap, :, lanes(chunk)]
                for j in range(TILE):
                    column = j + sign * (col_tap - REACH)
                    if 0 <= column < TILE:
                        out[j] = out[j] + row[column] * weight
    return out


def set_taps(taps_ref, depth_w_ref):
    taps = depth_w_ref[...].astype(f32)
    for k in range(KERNEL * KERNEL):
        taps_ref[k] = jnp.broadcast_to(taps[k : k + 1], (TILE, WIDTH))


def in_hbm(x):
    return pltpu.with_memory_space_constraint(x, pltpu.HBM)


class Copies:
    def __init__(self, sems):
        self.sems, self.made = sems, []

    def start(self, source, target):
        copy = pltpu.make_async_copy(source, target, self.sems.at[len(self.made)])
        self.made.append(copy)
        copy.start()
        return copy


def forward_kernel(
    count_ref, patches_ref, stem_w_hbm, depth_w_hbm, gain_ref, up_hbm, down_hbm, layer_ref,
    stem_hbm, centred_hbm, hidden_hbm, inv_ref, feat_hbm,
    stem_w_ref, depth_w_ref, up_ref, down_ref, stem_ref, centred_ref, half_ref, hidden_ref,
    projected_ref, feat_ref, taps_ref, field_ref, mixed_ref, normed_ref, act_ref, pool_ref, last_ref,
    sems,
):
    copies = Copies(sems)
    stem_w_in = copies.start(stem_w_hbm, stem_w_ref)
    depth_w_in = copies.start(depth_w_hbm, depth_w_ref)
    up_in = copies.start(up_hbm, up_ref)
    down_in = copies.start(down_hbm, down_ref)
    outs = []
    stem_w_in.wait()
    stem = jnp.dot(patches_ref[...], stem_w_ref[...], preferred_element_type=f32).astype(bf16)
    stem_ref[...] = stem
    outs.append(copies.start(stem_ref, stem_hbm))
    field_ref[...] = stem.astype(f32)
    depth_w_in.wait()
    set_taps(taps_ref, depth_w_ref)
    gain = gain_ref[...]

    def norm(at):
        row = mixed_ref[at, :]
        deviation = row - jnp.mean(row, axis=1, keepdims=True)
        inv_std = lax.rsqrt(jnp.mean(deviation * deviation, axis=1, keepdims=True) + epsilon)
        centred = deviation * inv_std
        centred_ref[at, :] = centred
        inv_ref[at, :] = jnp.broadcast_to(inv_std, (2 * TILE, LANES))
        normed_ref[at, :] = (centred * gain).astype(bf16)

    for i in range(TILE):
        for chunk in range(CHUNKS):
            out = depthwise_row(field_ref, taps_ref, chunk, 1, i)
            for j in range(TILE):
                mixed_ref[place_rows(i, j), lanes(chunk)] = out[j]
        for at in range(i * 64, i * 64 + 64, 16):
            norm(slice(at, at + 16))
    for chunk in range(CHUNKS):
        out = depthwise([field_ref[last_rows(i), lanes(chunk)] for i in range(TILE)], taps_ref, chunk, 1)
        for i in range(TILE):
            mixed_ref[last_rows(i), lanes(chunk)] = out[i]
    for at in range(LEAD_ROWS, POSITIONS, 16):
        norm(slice(at, at + 16))
    outs.append(copies.start(centred_ref, centred_hbm))
    up_in.wait()
    normed = normed_ref[...]
    for n in range(0, INNER, 256):
        hidden_ref[:, n : n + 256] = jnp.dot(
            normed, up_ref[:, n : n + 256], preferred_element_type=f32
        )

    def activate(r, carry):
        at = pl.ds(pl.multiple_of(r * 16, 16), 16)
        v = hidden_ref[at, :]
        half_ref[at, :] = v.astype(bf16)
        t = jnp.tanh(GELU_A * (v + GELU_B * (v * v * v)))
        act_ref[at, :] = (0.5 * v * (1.0 + t)).astype(bf16)
        return carry

    lax.fori_loop(0, POSITIONS // 16, activate, 0, unroll=4)
    outs.append(copies.start(half_ref, hidden_hbm))
    down_in.wait()
    projected_ref[...] = jnp.dot(act_ref[...], down_ref[...], preferred_element_type=f32)
    layer = layer_ref[...]
    count = count_ref[0, 0]

    keep = jnp.where(lax.broadcasted_iota(jnp.int32, (LEAD, WIDTH), 0) < count, 0.25, 0.0)

    def block(at):
        return field_ref[at, :] + layer * projected_ref[at, :]

    for f in range(FEAT_TILE):
        i, j = 2 * (f // 4), 2 * (f % 4)
        total = block(place_rows(i, j)) + block(place_rows(i, j + 1))
        total += block(place_rows(i + 1, j)) + block(place_rows(i + 1, j + 1))
        pool_ref[f * LEAD : (f + 1) * LEAD, :] = total * keep
    keep_last = jnp.where(count == SLOTS, 0.25, 0.0).astype(f32)
    for pair in range(TILE // 2):
        total = block(last_rows(2 * pair)) + block(last_rows(2 * pair + 1))
        total = (total + pltpu.roll(total, TILE - 1, 0)) * keep_last
        for chunk in range(CHUNKS):
            last_ref[chunk, pair * TILE : (pair + 1) * TILE, :] = total[:, lanes(chunk)]
    for chunk in range(CHUNKS):
        pool_ref[LEAD * FEAT_TILE :, lanes(chunk)] = last_ref[chunk, pl.ds(0, FEAT_TILE, stride=2), :]
    row = lax.broadcasted_iota(jnp.int32, (BLOCK_ROWS, BLOCK_ROWS), 0)
    col = lax.broadcasted_iota(jnp.int32, (BLOCK_ROWS, BLOCK_ROWS), 1)
    tile, f = lax.shift_right_logical(row, 4), row & 15
    order = jnp.where(col == jnp.where(tile < LEAD, f * LEAD + tile, LEAD * FEAT_TILE + f), 1.0, 0.0)
    feat_ref[...] = jnp.dot(
        order.astype(bf16), pool_ref[...].astype(bf16), preferred_element_type=f32
    ).astype(bf16)
    for d in range(N_DEC):
        outs.append(copies.start(feat_ref, feat_hbm.at[d]))
    for out in outs:
        out.wait()


def forward(count, patches, stem_w, depth_w, gain, up, down, layer):
    vmem = pl.BlockSpec(memory_space=pltpu.VMEM)
    smem = pl.BlockSpec(memory_space=pltpu.SMEM)
    hbm = pl.BlockSpec(memory_space=pltpu.HBM)
    stored = (
        ((POSITIONS, WIDTH), bf16),
        ((POSITIONS, WIDTH), f32),
        ((POSITIONS, INNER), bf16),
    )
    inv = jax.ShapeDtypeStruct((POSITIONS, LANES), f32)
    return pl.pallas_call(
        forward_kernel,
        out_shape=[pltpu.HBM(*shape) for shape in stored] + [inv, pltpu.HBM((N_DEC, BLOCK_ROWS, WIDTH), bf16)],
        in_specs=[smem, vmem, hbm, hbm, vmem, hbm, hbm, vmem],
        out_specs=[hbm, hbm, hbm, vmem, hbm],
        scratch_shapes=[
            pltpu.VMEM((PATCH_CH, WIDTH), bf16),
            pltpu.VMEM((KERNEL * KERNEL, WIDTH), bf16),
            pltpu.VMEM((WIDTH, INNER), bf16),
            pltpu.VMEM((INNER, WIDTH), bf16),
            *[pltpu.VMEM(*shape) for shape in stored],
            pltpu.VMEM((POSITIONS, INNER), f32),
            pltpu.VMEM((POSITIONS, WIDTH), f32),
            pltpu.VMEM((BLOCK_ROWS, WIDTH), bf16),
            pltpu.VMEM((KERNEL * KERNEL, TILE, WIDTH), f32),
            pltpu.VMEM((POSITIONS, WIDTH), f32),
            pltpu.VMEM((POSITIONS, WIDTH), f32),
            pltpu.VMEM((POSITIONS, WIDTH), bf16),
            pltpu.VMEM((POSITIONS, INNER), bf16),
            pltpu.VMEM((BLOCK_ROWS, WIDTH), f32),
            pltpu.VMEM((CHUNKS, TILE // 2 * TILE, LANES), f32),
            pltpu.SemaphoreType.DMA((18,)),
        ],
        compiler_params=pltpu.CompilerParams(vmem_limit_bytes=VMEM_BYTES),
        cost_estimate=pl.CostEstimate(
            flops=4 * POSITIONS * WIDTH * INNER, bytes_accessed=8 << 20, transcendentals=0
        ),
        name="block_forward",
    )(count, patches, in_hbm(stem_w), in_hbm(depth_w), gain, in_hbm(up), in_hbm(down), layer)


def rows_times_rows(a, b):
    return lax.dot_general(a, b, (((1,), (1,)), ((), ())), preferred_element_type=f32)


def over_positions(a, b):
    return lax.dot_general(a, b, (((0,), (0,)), ((), ())), preferred_element_type=f32)


def rows_sum(x):
    return jnp.sum(x.reshape(-1, TILE, WIDTH), axis=0)


def backward_kernel(
    place_ref, own_ref, other_ref, patches_ref, stem_hbm, centred_hbm, hidden_hbm,
    inv_ref, depth_w_hbm, gain_ref, up_hbm, down_hbm, layer_ref,
    mine_hbm, theirs_hbm, spans_ref,
    stem_ref, centred_ref, hidden_ref, depth_w_ref, up_ref, down_ref, packed_ref,
    taps_ref, embed_ref, block_ref, proj_ref, act_ref, work_ref, ghid_ref, normed_ref, field_ref,
    mixed_ref, gstem_ref, taps_sum_ref, scale_sum_ref, tails_ref, sems,
):
    copies = Copies(sems)
    y_here, core_here = place_ref[0], place_ref[1]
    dec_here = 2 * y_here + core_here
    down_in = copies.start(down_hbm, down_ref)
    hidden_in = copies.start(hidden_hbm, hidden_ref)
    up_in = copies.start(up_hbm, up_ref)
    centred_in = copies.start(centred_hbm, centred_ref)
    depth_w_in = copies.start(depth_w_hbm, depth_w_ref)
    stem_in = copies.start(stem_hbm, stem_ref)
    outs = []
    layer = layer_ref[...]
    gain = gain_ref[...]
    scale_sum_ref[...] = jnp.zeros((TILE, WIDTH), f32)
    embed_ref[SEQ:, :] = jnp.zeros((16, WIDTH), bf16)
    for used in (STEM_AT + CHUNKS * PATCH_CH, SMALL_AT + CHUNKS * SMALL_ROWS):
        end = HALF_ROWS if used < HALF_ROWS else PACK_ROWS
        packed_ref[used:end, :] = jnp.zeros((end - used, LANES), bf16)
    counts, gaps = [None] * N_DEC, [None] * N_DEC
    for y in range(N_DEC // 2):
        for k, source in ((core_here, own_ref), (1 - core_here, other_ref)):
            to = pl.ds(pl.multiple_of((2 * y + k) * SHARD, 16), SHARD)
            embed_ref[to, :] = source[y, :SHARD, :]
            tails_ref[k, y] = source[y, SHARD:, :]
        for core in range(2):
            tail = tails_ref[core, y, :, :LANES].astype(f32)
            counts[2 * y + core] = tail[0, 0].astype(jnp.int32)
            gaps[2 * y + core] = tail[0, 1].astype(jnp.int32)
    at, own_offset, count = jnp.int32(0), jnp.int32(0), jnp.int32(0)
    for d in range(N_DEC):
        start = at + gaps[d]
        spans_ref[d] = start
        spans_ref[N_DEC + d] = counts[d]
        own_offset = jnp.where(dec_here == d, start, own_offset)
        count = jnp.where(dec_here == d, counts[d], count)
        at = start + FEAT_TILE * counts[d]

    base = lax.div(own_offset, 16)
    row = lax.broadcasted_iota(jnp.int32, (POSITIONS, BLOCK_ROWS + 16), 0)
    col = lax.broadcasted_iota(jnp.int32, (POSITIONS, BLOCK_ROWS + 16), 1)
    tile = jnp.where(row < LEAD_ROWS, row & (LEAD - 1), LEAD)
    spot = jnp.where(row < LEAD_ROWS, lax.shift_right_logical(row, 3), row - LEAD_ROWS)
    feat = lax.shift_right_logical(spot, 4) * 4 + (lax.shift_right_logical(spot, 1) & 3)
    hit = (col == tile * FEAT_TILE + feat + (own_offset - 16 * base)) & (tile < count)
    pick = jnp.where(hit, 0.25, 0.0).astype(bf16)
    window = embed_ref[pl.ds(pl.multiple_of(base * 16, 16), BLOCK_ROWS + 16), :]
    block = jnp.dot(pick, window, preferred_element_type=f32)
    block_ref[...] = block
    proj_ref[...] = (block * layer).astype(bf16)
    proj = proj_ref[...]
    down_in.wait()
    for n in range(0, INNER, 256):
        work_ref[:, n : n + 256] = rows_times_rows(proj, down_ref[n : n + 256, :])

    hidden_in.wait()

    def activate(r, carry):
        at = pl.ds(pl.multiple_of(r * 16, 16), 16)
        v = hidden_ref[at, :].astype(f32)
        square = v * v
        t = jnp.tanh(GELU_A * (v + GELU_B * (square * v)))
        half = 0.5 * (1.0 + t)
        act_ref[at, :] = (v * half).astype(bf16)
        slope = half + (0.5 * GELU_A) * v * (1.0 - t * t) * (1.0 + (3.0 * GELU_B) * square)
        ghid_ref[at, :] = (work_ref[at, :] * slope).astype(bf16)
        return carry

    lax.fori_loop(0, POSITIONS // 16, activate, 0, unroll=4)
    up_in.wait()
    work_ref[:, :WIDTH] = rows_times_rows(ghid_ref[...], up_ref[...])
    centred_in.wait()
    stem_in.wait()
    depth_w_in.wait()
    set_taps(taps_ref, depth_w_ref)
    field_ref[...] = stem_ref[...].astype(f32)

    def unnorm(r, carry):
        at = pl.ds(pl.multiple_of(r * 16, 16), 16)
        grad = work_ref[at, :WIDTH]
        centred = centred_ref[at, :]
        normed_ref[at, :] = (centred * gain).astype(bf16)
        scaled = grad * gain
        mean = jnp.mean(scaled, axis=1, keepdims=True)
        mean_c = jnp.mean(scaled * centred, axis=1, keepdims=True)
        mixed_ref[at, :] = (scaled - mean - centred * mean_c) * inv_ref[at, :1]
        return carry + rows_sum(grad * centred)

    gain_sum = lax.fori_loop(0, POSITIONS // 16, unnorm, jnp.zeros((TILE, WIDTH), f32), unroll=6)

    def down_part(n):
        term = over_positions(act_ref[:, n : n + 256], proj)
        scale_sum_ref[...] += rows_sum(term * down_ref[n : n + 256, :].astype(f32))
        term = term.astype(bf16)
        for chunk in range(CHUNKS):
            to = DOWN_AT + chunk * INNER + n
            packed_ref[to : to + 256, :] = term[:, lanes(chunk)]

    def up_part(n):
        term = over_positions(normed_ref[...], ghid_ref[:, n : n + 256]).astype(bf16)
        for k in range(2):
            to = UP_AT + (n // LANES + k) * WIDTH
            packed_ref[to : to + WIDTH, :] = term[:, lanes(k)]

    def taps_term(chunk, row_tap):
        sums = [jnp.zeros((LEAD, LANES), f32)] * KERNEL
        for i in range(TILE):
            source = i + row_tap - REACH
            if 0 <= source < TILE:
                row = [field_ref[place_rows(source, j), lanes(chunk)] for j in range(TILE)]
                for j in range(TILE):
                    grad = mixed_ref[place_rows(i, j), lanes(chunk)]
                    for col_tap in range(KERNEL):
                        column = j + col_tap - REACH
                        if 0 <= column < TILE:
                            sums[col_tap] = sums[col_tap] + row[column] * grad
        for col_tap in range(KERNEL):
            taps_sum_ref[row_tap * KERNEL + col_tap, :, lanes(chunk)] = sums[col_tap]

    def unmix_row(chunk, i):
        inner = depthwise_row(mixed_ref, taps_ref, chunk, -1, i)
        for j in range(0, TILE, 2):
            at = slice((i * TILE + j) * LEAD, (i * TILE + j + 2) * LEAD)
            pair = jnp.concatenate([inner[j], inner[j + 1]], axis=0)
            gstem_ref[at, lanes(chunk)] = (block_ref[at, lanes(chunk)] + pair).astype(bf16)

    def unmix_last(chunk):
        grads = [mixed_ref[last_rows(i), lanes(chunk)] for i in range(TILE)]
        stem = [field_ref[last_rows(i), lanes(chunk)] for i in range(TILE)]
        for col_tap in range(KERNEL):
            moved = column_shift(stem, col_tap - REACH)
            for row_tap in range(KERNEL):
                total = None
                for i in range(TILE):
                    source = i + row_tap - REACH
                    if 0 <= source < TILE:
                        part = moved[source] * grads[i]
                        total = part if total is None else total + part
                taps_sum_ref[row_tap * KERNEL + col_tap, :, lanes(chunk)] += total
        inner = depthwise(grads, taps_ref, chunk, -1)
        for i in range(0, TILE, 2):
            at = slice(LEAD_ROWS + i * TILE, LEAD_ROWS + (i + 2) * TILE)
            pair = jnp.concatenate([inner[i], inner[i + 1]], axis=0)
            gstem_ref[at, lanes(chunk)] = (block_ref[at, lanes(chunk)] + pair).astype(bf16)

    for n in range(0, INNER, 256):
        up_part(n)
        down_part(n)
    for core, target in ((core_here, mine_hbm), (1 - core_here, theirs_hbm)):
        at = pl.ds(pl.multiple_of(core * HALF_ROWS, 16), LATE_AT)
        outs.append(copies.start(packed_ref.at[at], target.at[:LATE_AT]))
    for chunk in range(CHUNKS):
        for row_tap in range(KERNEL):
            taps_term(chunk, row_tap)
        for i in range(TILE):
            unmix_row(chunk, i)
    for chunk in range(CHUNKS):
        unmix_last(chunk)
    stem_term = over_positions(patches_ref[...], gstem_ref[...]).astype(bf16)
    scale_row = jnp.sum(scale_sum_ref[...], axis=0, keepdims=True) / layer
    small = jnp.concatenate(
        [
            jnp.sum(taps_sum_ref[...], axis=1),
            scale_row,
            jnp.sum(gain_sum, axis=0, keepdims=True),
            jnp.zeros((SMALL_ROWS - KERNEL * KERNEL - 2, WIDTH), f32),
        ],
        axis=0,
    ).astype(bf16)
    for chunk in range(CHUNKS):
        to = STEM_AT + chunk * PATCH_CH
        packed_ref[to : to + PATCH_CH, :] = stem_term[:, lanes(chunk)]
        to = SMALL_AT + chunk * SMALL_ROWS
        packed_ref[to : to + SMALL_ROWS, :] = small[:, lanes(chunk)]
    for k, target in ((core_here, mine_hbm), (1 - core_here, theirs_hbm)):
        at = pl.ds(pl.multiple_of(k * HALF_ROWS + LATE_AT, 16), HALF_ROWS - LATE_AT)
        outs.append(copies.start(packed_ref.at[at], target.at[LATE_AT:]))
    for out in outs:
        out.wait()


def backward(place, own, other, patches, stored, depth_w, gain, up, down, layer):
    vmem = pl.BlockSpec(memory_space=pltpu.VMEM)
    smem = pl.BlockSpec(memory_space=pltpu.SMEM)
    hbm = pl.BlockSpec(memory_space=pltpu.HBM)
    return pl.pallas_call(
        backward_kernel,
        out_shape=[
            pltpu.HBM((HALF_ROWS, LANES), bf16),
            pltpu.HBM((HALF_ROWS, LANES), bf16),
            jax.ShapeDtypeStruct((2 * N_DEC,), jnp.int32),
        ],
        in_specs=[smem, vmem, vmem, vmem, hbm, hbm, hbm, vmem, hbm, vmem, hbm, hbm, vmem],
        out_specs=[hbm, hbm, smem],
        scratch_shapes=[
            pltpu.VMEM((POSITIONS, WIDTH), bf16),
            pltpu.VMEM((POSITIONS, WIDTH), f32),
            pltpu.VMEM((POSITIONS, INNER), bf16),
            pltpu.VMEM((KERNEL * KERNEL, WIDTH), bf16),
            pltpu.VMEM((WIDTH, INNER), bf16),
            pltpu.VMEM((INNER, WIDTH), bf16),
            pltpu.VMEM((PACK_ROWS, LANES), bf16),
            pltpu.VMEM((KERNEL * KERNEL, TILE, WIDTH), f32),
            pltpu.VMEM((SEQ + 16, WIDTH), bf16),
            pltpu.VMEM((POSITIONS, WIDTH), f32),
            pltpu.VMEM((POSITIONS, WIDTH), bf16),
            pltpu.VMEM((POSITIONS, INNER), bf16),
            pltpu.VMEM((POSITIONS, INNER), f32),
            pltpu.VMEM((POSITIONS, INNER), bf16),
            pltpu.VMEM((POSITIONS, WIDTH), bf16),
            pltpu.VMEM((POSITIONS, WIDTH), f32),
            pltpu.VMEM((POSITIONS, WIDTH), f32),
            pltpu.VMEM((POSITIONS, WIDTH), bf16),
            pltpu.VMEM((KERNEL * KERNEL, TILE, WIDTH), f32),
            pltpu.VMEM((TILE, WIDTH), f32),
            pltpu.VMEM((2, N_DEC // 2, 16, WIDTH), bf16),
            pltpu.SemaphoreType.DMA((24,)),
        ],
        compiler_params=pltpu.CompilerParams(vmem_limit_bytes=VMEM_BYTES),
        cost_estimate=pl.CostEstimate(
            flops=8 * POSITIONS * WIDTH * INNER, bytes_accessed=10 << 20, transcendentals=0
        ),
        name="block_backward",
    )(
        place, own, other, patches, *map(in_hbm, stored[:3]), stored[3], in_hbm(depth_w), gain,
        in_hbm(up), in_hbm(down), layer,
    )


def place_kernel(place_ref, spans_ref, feat_ref, out_ref, rows_ref):
    base = (2 * place_ref[0] + place_ref[1]) * SHARD
    rows_ref[...] = jnp.zeros((FEAT_TILE + SHARD + FEAT_TILE, WIDTH), f32)

    def one(k, carry):
        d = lax.div(k, SLOTS)
        j = k - d * SLOTS
        to = spans_ref[d] + FEAT_TILE * j - base

        @pl.when((j < spans_ref[N_DEC + d]) & (to > -FEAT_TILE) & (to < SHARD))
        def _():
            at = pl.ds(pl.multiple_of(j * FEAT_TILE, FEAT_TILE), FEAT_TILE)
            chunk = lax.div(to + FEAT_TILE, 16)
            row = lax.broadcasted_iota(jnp.int32, (32, FEAT_TILE), 0)
            col = lax.broadcasted_iota(jnp.int32, (32, FEAT_TILE), 1)
            pick = jnp.where(row == col + (to + FEAT_TILE - 16 * chunk), 1.0, 0.0).astype(bf16)
            window = pl.ds(pl.multiple_of(chunk * 16, 16), 32)
            rows_ref[window, :] += jnp.dot(pick, feat_ref[d, at, :], preferred_element_type=f32)

        return carry

    lax.fori_loop(0, N_DEC * SLOTS, one, 0)
    out_ref[...] = rows_ref[FEAT_TILE : FEAT_TILE + SHARD, :].astype(bf16)


def place_features(place, spans, feat):
    vmem = pl.BlockSpec(memory_space=pltpu.VMEM)
    smem = pl.BlockSpec(memory_space=pltpu.SMEM)
    return pl.pallas_call(
        place_kernel,
        out_shape=jax.ShapeDtypeStruct((SHARD, WIDTH), bf16),
        in_specs=[smem, smem, vmem],
        out_specs=vmem,
        scratch_shapes=[pltpu.VMEM((FEAT_TILE + SHARD + FEAT_TILE, WIDTH), f32)],
        compiler_params=pltpu.CompilerParams(vmem_limit_bytes=VMEM_BYTES),
        name="place_features",
    )(place, spans, feat)


def unpack_kernel(
    place_ref, own_ref, other_ref, stem_ref, depth_ref, gain_ref, up_ref, down_ref, scale_ref, rows_ref
):
    core = place_ref[1]
    factor = 1.0 / math.sqrt(N_OWNERS * MEAN_TILES * FEAT_TILE)
    rows_ref[pl.ds(pl.multiple_of(core * HALF_ROWS, 16), HALF_ROWS), :] = own_ref[...]
    rows_ref[pl.ds(pl.multiple_of((1 - core) * HALF_ROWS, 16), HALF_ROWS), :] = other_ref[...]

    def piece(at, count):
        return rows_ref[at : at + count, :].astype(f32) * factor

    for k in range(INNER // LANES):
        up_ref[:, lanes(k)] = piece(UP_AT + k * WIDTH, WIDTH)
    for chunk in range(CHUNKS):
        down_ref[:, lanes(chunk)] = piece(DOWN_AT + chunk * INNER, INNER)
        stem_ref[:, lanes(chunk)] = piece(STEM_AT + chunk * PATCH_CH, PATCH_CH)
        small = piece(SMALL_AT + chunk * SMALL_ROWS, SMALL_ROWS)
        taps = KERNEL * KERNEL
        depth_ref[:, lanes(chunk)] = small[:taps]
        scale_ref[lanes(chunk)] = small[taps]
        gain_ref[lanes(chunk)] = small[taps + 1]


def unpack(place, own, other):
    vmem = pl.BlockSpec(memory_space=pltpu.VMEM)
    smem = pl.BlockSpec(memory_space=pltpu.SMEM)
    shapes = (
        (PATCH_CH, WIDTH),
        (KERNEL * KERNEL, WIDTH),
        (WIDTH,),
        (WIDTH, INNER),
        (INNER, WIDTH),
        (WIDTH,),
    )
    return pl.pallas_call(
        unpack_kernel,
        out_shape=[jax.ShapeDtypeStruct(shape, f32) for shape in shapes],
        in_specs=[smem, vmem, vmem],
        out_specs=[vmem] * 6,
        scratch_shapes=[pltpu.VMEM((PACK_ROWS, LANES), bf16)],
        compiler_params=pltpu.CompilerParams(vmem_limit_bytes=VMEM_BYTES),
        name="unpack_terms",
    )(place, own, other)


def prepare_kernel(count_hbm, gap_hbm, embed_hbm, out_hbm, rows_ref, count_ref, gap_ref, sems):
    copies = Copies(sems)
    count_in = copies.start(count_hbm, count_ref)
    gap_in = copies.start(gap_hbm, gap_ref)
    rows_in = copies.start(embed_hbm.at[0], rows_ref.at[:SHARD])
    count_in.wait()
    gap_in.wait()
    lane = lax.broadcasted_iota(jnp.int32, (16, WIDTH), 1)
    count, gap = count_ref[0, 0].astype(f32), gap_ref[0, 0].astype(f32)
    rows_ref[SHARD:, :] = jnp.where(lane == 0, count, jnp.where(lane == 1, gap, 0.0)).astype(bf16)
    rows_in.wait()
    outs = [copies.start(rows_ref, out_hbm.at[y]) for y in range(N_DEC // 2)]
    for out in outs:
        out.wait()


def prepare(tile_counts, text_gaps, embed_grad):
    hbm = pl.BlockSpec(memory_space=pltpu.HBM)
    return pl.pallas_call(
        prepare_kernel,
        out_shape=pltpu.HBM((N_DEC // 2, SHARD + 16, WIDTH), bf16),
        in_specs=[pl.BlockSpec(memory_space=pl.ANY)] * 2 + [hbm],
        out_specs=hbm,
        scratch_shapes=[
            pltpu.VMEM((SHARD + 16, WIDTH), bf16),
            pltpu.SMEM((1, 1), jnp.int32),
            pltpu.SMEM((1, 1), jnp.int32),
            pltpu.SemaphoreType.DMA((8,)),
        ],
        compiler_params=pltpu.CompilerParams(vmem_limit_bytes=VMEM_BYTES),
        name="prepare_rows",
    )(tile_counts, text_gaps, in_hbm(embed_grad))


def swap_blocks(blocks, axes, groups=None):
    return lax.all_to_all(blocks, axes, 0, 0, axis_index_groups=groups, tiled=True)


def sum_blocks(blocks):
    return jnp.sum(blocks.astype(f32), axis=0).astype(bf16)


def spread(block, copies):
    return jnp.broadcast_to(block[None], (copies,) + block.shape)


def swap_cores(x):
    return lax.ppermute(x, "core", [(0, 1), (1, 0)])


def sum_all(half, beside):
    part = sum_blocks(swap_blocks(half.reshape(32, HALF_ROWS // 32, LANES), BLOCK, BLOCKS))
    part = sum_blocks(swap_blocks(spread(part, 8), ("pair", "side"), ACROSS))
    part, beside = lax.optimization_barrier((part, beside))
    return swap_blocks(spread(part, 32), BLOCK, BLOCKS).reshape(HALF_ROWS, LANES), beside


def order_patches(tiles):
    patches = tiles.reshape(SLOTS, TILE * TILE, PATCH_CH)
    lead = patches[:LEAD].transpose(1, 0, 2).reshape(LEAD_ROWS, PATCH_CH)
    return jnp.concatenate([lead, patches[LEAD]])


def on_device(
    pixels,
    tile_counts,
    text_gaps,
    stem_weight,
    depth_weight,
    norm_gain,
    up_weight,
    down_weight,
    layer_scale,
    embed_grad,
):
    place = jnp.stack([lax.axis_index("y"), lax.axis_index("core")]).astype(jnp.int32)
    gain = norm_gain.reshape(1, WIDTH)
    layer = layer_scale.reshape(1, WIDTH)
    patches = order_patches(pixels[0])
    own = swap_blocks(prepare(tile_counts, text_gaps, embed_grad), "y")
    *stored, feat = forward(
        tile_counts, patches, stem_weight, depth_weight, gain, up_weight, down_weight, layer
    )
    own, feat, place = lax.optimization_barrier((own, feat, place))
    other = swap_cores(own)
    feats = swap_blocks(feat, DEC)
    mine, theirs, spans = backward(
        place, own, other, patches, stored, depth_weight, gain, up_weight, down_weight, layer
    )
    theirs, feats = lax.optimization_barrier((theirs, feats))
    half = (mine.astype(f32) + swap_cores(theirs).astype(f32)).astype(bf16)
    sequence = place_features(place, spans, feats)
    half, sequence = sum_all(half, sequence)
    stem, depth, gain_grad, up, down, scale = unpack(place, half, swap_cores(half))
    return sequence[None], stem, depth, gain_grad, up, down, scale


def solution(mesh):
    fine = Mesh(mesh.devices.reshape(4, 8, 2, 4, 2), ("x", "pair", "side", "y", "core"))
    return jax.shard_map(
        on_device,
        mesh=fine,
        in_specs=(
            P(DEC, ENC, None),
            P(DEC, ENC),
            P(DEC, ENC),
            P(),
            P(),
            P(),
            P(),
            P(),
            P(),
            P(ENC, DEC, None),
        ),
        out_specs=(P(ENC, DEC, None), P(), P(), P(), P(), P(), P()),
        check_vma=False,
    )
```
